512 devices in a mesh: slab: 32 (over x, y, core), grp: 16 (over z).
Axes of the slice: x: 4, y: 4, z: 16, core: 2. Of those that a mesh axis runs over, the one named last changes fastest.
Arguments:
- fields: bfloat16 [27, 1048576], P(None, ('slab', 'grp')), may hold values from -5 to 5
- spline: bfloat16 [3, 8, 4, 2097152], P(None, None, None, ('slab', 'grp')), may hold values from -4 to 4
- measured: float32 [3, 2097152], P(None, ('slab', 'grp')), may hold values from -6 to 6
- confidence: float32 [2097152], P(('slab', 'grp')), may hold values from 0.05 to 3
- block_ids: int32 [32768, 4], P(('slab', 'grp')), may hold values from 0 to 63, all different within a row
- live: int32 [32768], P(('slab', 'grp')), may hold values from 1 to 4
- owners: int32 [2097152, 1], P(('slab', 'grp')), may hold values from 0 to 511; in each aligned block of 4096 rows (0 to 4095, 4096 to 8191, ...) at most 16 rows name the same one
Outputs:
- received: float32 [8, 4194304], P(None, ('slab', 'grp'))
- update: float32 [8], replicated
The draws below stay inside these ranges and needn't reach their ends.
Inputs may be any that keep to these rules, and one draw needn't show every extreme that they name: `block_ids`: each row names 4 different voxel blocks of its own slab. `owners`: among the 4096 subsets of one device, at most 16 have the same owner, and some owner gets exactly 16 of them.
All inputs are finite; a program needn't handle non-finite values.
Results may differ from the reference program's by a relative error of at most 0.0018.
Values may be sent and summed in bfloat16 or wider, within the bound.
A program may use at most 128 MiB of HBM per device.

```python
import math
import jax
import jax.numpy as jnp
import numpy as np
from jax import lax

PARAMS = 8
EDGE = 8
SUBS = 64
K = 4
SB_DEV = 64
VB_DEV = 4
BLK = 512
PEERS = 512
S_DEV = 4096
NSB = 32768
NSUB = 2097152
NVOX = 1048576
SLAB_BLK = 64
CAP = 16
N_SLAB = 32
N_GRP = 16


def draw_fields(key, part):
    leaning = jax.random.uniform(jax.random.fold_in(key, 11), (PARAMS,), jnp.float32, -0.7, 0.7)
    base_rows = jnp.clip(jax.random.normal(jax.random.fold_in(key, 12), (3, NVOX), jnp.float32), -5.0, 5.0)
    rough_rows = jnp.clip(jax.random.normal(jax.random.fold_in(key, 13), (3 * PARAMS, NVOX), jnp.float32), -5.0, 5.0)
    keep_share = jnp.sqrt(1.0 - leaning * leaning)
    sensitivity = leaning[:, None, None] * base_rows[None, :, :] + keep_share[:, None, None] * rough_rows.reshape(PARAMS, 3, NVOX)
    joined = jnp.concatenate([base_rows, sensitivity.reshape(3 * PARAMS, NVOX)], axis=0)
    return jnp.clip(joined, -5.0, 5.0).astype(jnp.bfloat16)


def draw_confidence(key, part):
    position = jnp.arange(NSUB, dtype=jnp.float32) / (NSUB - 1)
    rising = 1.0 + 2.0 * position
    spread = jnp.exp(jax.random.uniform(key, (NSUB,), jnp.float32, math.log(0.1), 0.0))
    return rising * spread


def set_ends(array, own_key, low, largest):
    extent = array.shape
    place = [jax.random.randint(jax.random.fold_in(own_key, axis), (), 0, extent[axis]) for axis in range(len(extent))]
    array = array.at[tuple(place)].set(low)
    longest = extent.index(max(extent))
    place[longest] = (place[longest] + 1) % extent[longest]
    return array.at[tuple(place)].set(largest)


def block_levels(key, shape, pieces, smallest, largest):
    level, own = 1.0, jax.random.fold_in(key, 6)
    for dim, blocks in pieces:
        heights = jnp.exp(jax.random.uniform(jax.random.fold_in(own, dim), (blocks,), jnp.float32, smallest / len(pieces), largest / len(pieces)))
        level = level * jnp.repeat(heights, shape[dim] // blocks).reshape([-1 if axis == dim else 1 for axis in range(len(shape))])
    return level


def choose_distinct(key, rows, count, top, lift):
    sequence = jax.random.permutation(jax.random.fold_in(key, 1), count)
    pull = sequence
    for power in range(3):
        pull = pull * pull // count
    pull = pull * lift // count
    tickets = jax.random.randint(jax.random.fold_in(key, 2), (rows, count), 0, 4096) + pull
    fixed_rows = jax.random.permutation(jax.random.fold_in(key, 3), rows)[jnp.arange(count) % rows]
    tickets = jnp.where(jnp.arange(rows)[:, None] == fixed_rows[None, :], 1 << 14, tickets)
    priority = tickets * count + jnp.arange(count)
    return lax.top_k(priority.astype(jnp.int32), top)[1].astype(jnp.int32)


def routed_block(rng, own, number, rows, amount, top, reach, skew):
    order = jax.random.permutation(rng, amount)
    crowded, common = portions_of(amount, rows * top, reach, skew, True), portions_of(amount, rows * top, reach, skew, False)
    places = jnp.arange(amount)

    def named(lengths, turn):
        used = int((lengths > 0).sum())
        fixed = max(1, used // 4)
        moved = fixed + (places - fixed + turn * (used - fixed)) % max(1, amount - fixed)
        return jnp.zeros((amount,), jnp.int32).at[order[jnp.where(places < fixed, places, moved)]].set(jnp.asarray(lengths, jnp.int32))

    lengths = jnp.where(number % 4 == 0, named(crowded, number // 4), named(common, number - number // 4 - 1))
    mixed = jax.random.permutation(jax.random.fold_in(own, 3), amount)
    giver, taker = mixed[0:amount // 2 * 2:2], mixed[1:amount // 2 * 2:2]
    room = jnp.minimum(lengths[giver] - 1, reach - lengths[taker]) // 2
    room = jnp.where((giver == order[0]) | (taker == order[0]) | (lengths[taker] == 0), 0, jnp.maximum(room, 0))
    moved = jax.random.randint(jax.random.fold_in(own, 4), (amount // 2,), 0, 1 << 20) % (room + 1)
    lengths = lengths.at[giver].add(-moved).at[taker].add(moved)
    members = jnp.searchsorted(jnp.cumsum(lengths), jnp.arange(rows * top), side="right").astype(jnp.int32)
    grid = members.reshape(top, rows).T
    grid = grid[jax.random.permutation(jax.random.fold_in(own, 1), rows)]
    turn = jax.random.randint(jax.random.fold_in(own, 2), (rows, 1), 0, top)
    return jnp.take_along_axis(grid, (jnp.arange(top)[None, :] + turn) % top, axis=1)


def portions_of(number_of, total, bound, skew, full):
    portions = [(1 << 20) // math.isqrt(standing ** skew) + 1 for standing in range(1, number_of + 1)]
    largest = bound if full else min(bound, max(-(-total // number_of), total * portions[0] // sum(portions)))
    least = 1 if total - largest >= number_of - 1 else 0
    given, rest = [largest] + [least] * (number_of - 1), total - largest - least * (number_of - 1)
    while rest > 0:
        free = [i for i in range(1, number_of) if given[i] < largest] or [i for i in range(1, number_of) if given[i] < bound]
        pool, left = sum([portions[i] for i in free]), rest
        for i in free:
            extra = min(bound - given[i], max(1, left * portions[i] // pool), rest)
            given[i] = given[i] + extra
            rest = rest - extra
    return np.array(given)


def gaussian(own_key, shape, scale, most, cuts=(), kind=jnp.bfloat16):
    array = scale * jax.random.normal(own_key, shape, jnp.float32)
    if cuts:
        array = array * block_levels(own_key, shape, cuts, -0.22, 0.18)
    return jnp.clip(array, -most, most).astype(kind)


def setup_inputs(seed: int = 0) -> dict:
    key_of = jax.random.split(jax.random.key(seed), 8)
    fields = draw_fields(jax.random.fold_in(key_of[7], 71), 0)
    spline = gaussian(key_of[1], (3, EDGE, K, NSUB), 0.28, 4.0, ((3, 512),))
    measured = gaussian(key_of[2], (3, NSUB), 1.0, 6.0, ((1, 512),), jnp.float32)
    confidence = draw_confidence(jax.random.fold_in(key_of[7], 71), 0)
    block_ids = choose_distinct(key_of[4], NSB, SLAB_BLK, K, 0)
    live = set_ends(jax.random.randint(key_of[5], (NSB,), 1, K + 1), jax.random.fold_in(key_of[5], 1), 1, K).astype(jnp.int32)
    owners_keys = jax.random.split(jax.random.fold_in(key_of[6], 1), NSUB // S_DEV)
    owners_turns = jax.random.permutation(jax.random.fold_in(key_of[6], 3), NSUB // S_DEV)
    owners = jax.vmap(lambda own, number: routed_block(jax.random.fold_in(key_of[6], 2), own, number, S_DEV, PEERS, 1, CAP, 2))(owners_keys, owners_turns).reshape((NSUB, 1))
    return dict(fields=fields, spline=spline, measured=measured, confidence=confidence, block_ids=block_ids, live=live, owners=owners)


damping = 0.05

def build_tiles(spline_part, live_part):
    along_z = spline_part[0].astype(jnp.float32)
    along_y = spline_part[1].astype(jnp.float32)
    along_x = spline_part[2].astype(jnp.float32)
    edge_cells = along_z.shape[0]
    product = along_z[:, None, None] * along_y[None, :, None]
    product = product * along_x[None, None, :]
    product = product.reshape((edge_cells * edge_cells * edge_cells,) + along_z.shape[1:])
    slot_iota = lax.broadcasted_iota(jnp.int32, (along_z.shape[1], along_z.shape[2]), 0)
    keep_mask = (slot_iota < live_part[None, :]).astype(jnp.float32)
    return (product * keep_mask[None, :, :, None]).astype(jnp.bfloat16)

def local_normal(modelled, measured_rows, confidence_row, parameters):
    residual = measured_rows - modelled[0:3]
    flat_sens = modelled[3:].reshape(parameters, -1)
    weighted = jnp.broadcast_to(confidence_row[None, :], residual.shape).reshape(-1)
    hessian = jnp.einsum('ai,bi->ab', flat_sens, flat_sens * weighted[None, :], precision=lax.Precision.HIGHEST)
    gradient = jnp.dot(flat_sens, residual.reshape(-1) * weighted, precision=lax.Precision.HIGHEST)
    return (residual, hessian, gradient)

def solve_normal(hessian, gradient):
    damped = hessian + damping * jnp.diag(jnp.diag(hessian))
    factor = jnp.linalg.cholesky(damped)
    length = gradient.shape[0]
    forward = []
    for row_index in range(length):
        running = gradient[row_index]
        for col_index in range(row_index):
            running = running - factor[row_index, col_index] * forward[col_index]
        forward.append(running / factor[row_index, row_index])
    backward = [None] * length
    for row_index in reversed(range(length)):
        running = forward[row_index]
        for col_index in range(row_index + 1, length):
            running = running - factor[col_index, row_index] * backward[col_index]
        backward[row_index] = running / factor[row_index, row_index]
    return jnp.stack(backward)

def assemble(modelled_rows, residual, confidence_row, update):
    parameters = update.shape[0]
    sensitivity = modelled_rows[3:].reshape(parameters, 3, -1)
    predicted = jnp.einsum('acs,a->cs', sensitivity, update, precision=lax.Precision.HIGHEST)
    remaining = residual - predicted
    return jnp.concatenate([modelled_rows[0:3] + predicted, confidence_row[None, :] * remaining, confidence_row[None, :], confidence_row[None, :] * jnp.sum(remaining * remaining, axis=0, keepdims=True)], axis=0)

def place_slots(payload, destination, peer_count, capacity):
    subset_count = destination.shape[0]
    permutation = jnp.argsort(destination, stable=True).astype(jnp.int32)
    ordered = destination[permutation]
    run_start = jnp.searchsorted(ordered, ordered, side='left').astype(jnp.int32)
    rank_sorted = jnp.arange(subset_count, dtype=jnp.int32) - run_start
    rank_within = jnp.zeros((subset_count,), jnp.int32).at[permutation].set(rank_sorted)
    column = destination * capacity + rank_within
    return jnp.zeros((payload.shape[0], peer_count * capacity), payload.dtype).at[:, column].set(payload)

def reference(fields, spline, measured, confidence, block_ids, live, owners):
    peer_count = N_SLAB * N_GRP
    channels = fields.shape[0]
    blocks_all = fields.reshape(channels, peer_count * VB_DEV, BLK)

    def per_device(device):
        id_part = lax.dynamic_slice_in_dim(block_ids, device * SB_DEV, SB_DEV, 0)
        live_part = lax.dynamic_slice_in_dim(live, device * SB_DEV, SB_DEV, 0)
        spline_part = lax.dynamic_slice_in_dim(spline, device * S_DEV, S_DEV, 3).reshape(3, EDGE, K, SB_DEV, SUBS)
        measured_rows = lax.dynamic_slice_in_dim(measured, device * S_DEV, S_DEV, 1)
        confidence_row = lax.dynamic_slice_in_dim(confidence, device * S_DEV, S_DEV, 0)
        global_ids = (id_part + device // N_GRP * SLAB_BLK).astype(jnp.int32)
        picked = jnp.take(blocks_all, global_ids, axis=1).astype(jnp.float32)
        tile_set = build_tiles(spline_part, live_part).astype(jnp.float32)
        modelled = jnp.einsum('cnkv,vkns->cns', picked, tile_set, precision=lax.Precision.HIGHEST).reshape(channels, S_DEV)
        residual, hessian, gradient = local_normal(modelled, measured_rows, confidence_row, PARAMS)
        return (modelled, residual, hessian, gradient)
    modelled, residual, hessian, gradient = lax.map(per_device, jnp.arange(peer_count, dtype=jnp.int32))
    update = solve_normal(jnp.sum(hessian, axis=0), jnp.sum(gradient, axis=0))
    confidence_rows = confidence.reshape(peer_count, S_DEV)
    owner_rows = owners.reshape(peer_count, S_DEV)

    def finish(items):
        modelled_one, residual_one, confidence_one, owner_one = items
        payload = assemble(modelled_one, residual_one, confidence_one, update)
        return place_slots(payload, owner_one, peer_count, CAP)
    sent_rows = lax.map(finish, (modelled, residual, confidence_rows, owner_rows))
    received = sent_rows.reshape(peer_count, 8, peer_count, CAP).transpose(1, 2, 0, 3).reshape(8, peer_count * peer_count * CAP)
    return (received, update)
```

```python
import functools

import jax
import jax.numpy as jnp
from jax import lax
from jax.experimental import pallas as pl
from jax.experimental.pallas import tpu as pltpu
from jax.sharding import PartitionSpec as P

MESH = pl.DeviceIdType.MESH
F32 = jnp.float32
BF16 = jnp.bfloat16
DAMPING = 0.05

PARAMS = 8
COMPS = 3
CHANNELS = 27
ROWS = 32
BLOCKS = 4
PACKED = 112
BLK = 512
HALF = 256
SLOTS = 4
CAP = 16
GRP = 16
SLAB = 32
SUBSETS = 4096
TILES = 32
CHUNK = 256
CHUNKS = 16
PEERS = 512
HIGH = 64


def iota(shape, axis):
    return lax.broadcasted_iota(jnp.int32, shape, axis)


def split_two(value):
    upper = value.astype(BF16).astype(F32)
    return upper, (value - upper).astype(BF16).astype(F32)


def swap_chunks(value):
    sub, lane = iota((8, 128), 0), iota((8, 128), 1)
    for bit in range(3):
        step = 1 << bit
        sub_bit, lane_bit = (sub >> bit) & 1, (lane >> (4 + bit)) & 1
        upward = pltpu.roll(pltpu.roll(value, 16 * step, 1), 8 - step, 0)
        downward = pltpu.roll(pltpu.roll(value, 128 - 16 * step, 1), step, 0)
        value = jnp.where(sub_bit == lane_bit, value, jnp.where(sub_bit == 0, upward, downward))
    return value


def kernel(
    ids_ref, live_ref, fields_ref, spline_hbm, meas_ref, conf_ref, own_ref,
    out_ref, upd_ref,
    spline_ref, spline_sem, land, store, tiles, sp32, carry, upper_ref, unpack_ref,
    scatter_b, scatter_m, scatter_a, early_acc, sens, resid, norm_l, norm_r,
    red1, red2, early_out, early1, early2_out, early2, late_out, late1, late2_out, late2, flip,
    ag_send, ag_recv, r1s, r1r, r2s, r2r, e1s, e1r, e2s, e2r, d1s, d1r, d2s, d2r,
):
    me_s = lax.axis_index("slab")
    me_g = lax.axis_index("grp")
    right, left = lax.rem(me_g + 1, GRP), lax.rem(me_g + GRP - 1, GRP)

    barrier = pltpu.get_barrier_semaphore()

    @pl.loop(1, GRP)
    def _(j):
        pl.semaphore_signal(barrier, inc=1, device_id=(me_s, lax.rem(me_g + j, GRP)), device_id_type=MESH)

    @pl.loop(1, SLAB)
    def _(j):
        pl.semaphore_signal(barrier, inc=1, device_id=(lax.rem(me_s + j, SLAB), me_g), device_id_type=MESH)

    spline_copy = pltpu.make_async_copy(spline_hbm, spline_ref, spline_sem)
    spline_copy.start()

    row = iota((PACKED, CHANNELS), 0)
    channel = iota((PACKED, CHANNELS), 1)
    packed = None
    for j in range(BLOCKS):
        new = row - CHANNELS * j
        source = jnp.where(new < 24, 3 + 3 * (new & 7) + (new >> 3), new - 24)
        pick = (channel == source) & (new >= 0) & (new < CHANNELS)
        part = jnp.dot(
            jnp.where(pick, 1.0, 0.0).astype(BF16), fields_ref[:, j * BLK:(j + 1) * BLK], preferred_element_type=F32
        )
        packed = part if packed is None else packed + part
    packed = packed.astype(BF16)
    land[0, me_g] = packed[:, :HALF]
    land[1, me_g] = packed[:, HALF:]

    row, col = iota((CHUNK, CHUNK + 128), 0), iota((CHUNK, CHUNK + 128), 1)
    upper_ref[...] = jnp.where((row < col) | (col >= CHUNK), 1.0, 0.0).astype(BF16)
    row, col = iota((BLOCKS * ROWS, PACKED), 0), iota((BLOCKS * ROWS, PACKED), 1)
    unpack = jnp.zeros((BLOCKS * ROWS, PACKED), F32)
    for j in range(BLOCKS):
        inside = (row >= ROWS * j) & (row < ROWS * j + CHANNELS)
        unpack = jnp.where(inside & (col == row - (ROWS - CHANNELS) * j), 1.0, unpack)
    unpack_ref[...] = unpack.astype(BF16)
    carry[...] = jnp.zeros_like(carry)
    early_acc[...] = jnp.zeros_like(early_acc)
    late_out[...] = jnp.zeros_like(late_out)
    norm_r[...] = jnp.zeros_like(norm_r)

    def ring(direction, i, h, slot, target):
        return pltpu.make_async_remote_copy(
            src_ref=land.at[h, slot], dst_ref=land.at[h, slot],
            send_sem=ag_send.at[direction, i, h], recv_sem=ag_recv.at[direction, i, h],
            device_id=(me_s, target), device_id_type=MESH,
        )

    def unpack_slot(h, slot):
        rows = jnp.dot(unpack_ref[...], land[h, slot], preferred_element_type=F32).astype(BF16)
        store[h, pl.ds(BLOCKS * slot, BLOCKS)] = rows.reshape(BLOCKS, ROWS, HALF)

    def build_tile(t):
        lanes = pl.ds(pl.multiple_of(t * 128, 128), 128)
        for axis in range(3):
            part = spline_ref[axis, :, :, lanes].astype(F32)
            for e in range(8):
                sp32[axis, e * 4:(e + 1) * 4, :] = part[e]
        live_row = jnp.where(iota((8, 128), 1) < 64, live_ref[2 * t], live_ref[2 * t + 1])
        for k in range(SLOTS):
            along_z = sp32[0, pl.ds(k, 8, stride=4), :]
            along_y = sp32[1, pl.ds(k, 8, stride=4), :]
            along_x = sp32[2, pl.ds(k, 8, stride=4), :]
            along_z = jnp.where(live_row > k, along_z, 0.0)
            for z in range(8):
                face = along_z[z:z + 1, :] * along_y
                cells = (face[:, None, :] * along_x[None, :, :]).reshape(64, 128)
                start = (z // 4) * 1024 + k * HALF + (z % 4) * 64
                tiles[t, start:start + 64, :] = cells.astype(BF16)

    def place_chunk(j):
        lanes = pl.ds(pl.multiple_of(j * CHUNK, CHUNK), CHUNK)
        owner = own_ref[:, lanes]
        onehot = jnp.where(iota((PEERS, CHUNK), 0) == owner, 1.0, 0.0)
        counted = jnp.dot(onehot.astype(BF16), upper_ref[...], preferred_element_type=F32)
        before = carry[...]
        rank = jnp.sum(
            onehot * (counted[:, :CHUNK] + jnp.concatenate([before, before], axis=1)), axis=0, keepdims=True
        )
        carry[...] = before + counted[:, CHUNK:]
        low = ((owner >> 4) & 7) * CAP + rank.astype(jnp.int32)
        high = (owner & 15) * 4 + (owner >> 7)
        column = jnp.where(iota((128, CHUNK), 0) == low, 1.0, 0.0).T.astype(BF16)
        scatter_b[lanes, :] = column
        mask = jnp.where(iota((HIGH, CHUNK), 0) == high, 1.0, 0.0)
        scatter_m[:, lanes] = mask.astype(BF16)
        pieces = []
        for value in [meas_ref[c:c + 1, lanes] for c in range(COMPS)] + [conf_ref[:, lanes]]:
            pieces.append(split_two(value))
        stacked = jnp.concatenate(
            [(mask * pieces[c][part]).astype(BF16) for part in range(2) for c in range(4)], axis=0
        )
        early_acc[...] += jnp.dot(stacked, column, preferred_element_type=F32)

    pl.semaphore_wait(barrier, GRP + SLAB - 2)

    @pl.loop(0, CHUNKS)
    def _(j):
        i, h = j // 2, j % 2
        back, ahead = lax.rem(me_g + GRP - i, GRP), lax.rem(me_g + i, GRP)

        @pl.when(i > 0)
        def _():
            ring(0, i - 1, h, back, right).wait_recv()
            ring(1, i - 1, h, ahead, left).wait_recv()

        @pl.when((i < 7) | (h == 0))
        def _():
            ring(0, i, h, back, right).start()

        @pl.when((i < 7) | (h == 1))
        def _():
            ring(1, i, h, ahead, left).start()

        @pl.when(j == 0)
        def _():
            spline_copy.wait()

        unpack_slot(h, back)
        unpack_slot(h, ahead)
        build_tile(2 * j)
        build_tile(2 * j + 1)
        place_chunk(j)

    total = early_acc[0:4 * HIGH, :] + early_acc[4 * HIGH:, :]
    for c in range(4):
        for g in range(GRP):
            early_out[16 * g + 4 * c:16 * g + 4 * c + 4, :] = total[HIGH * c + 4 * g:HIGH * c + 4 * g + 4, :]

    opposite = lax.rem(me_g + 8, GRP)
    ring(0, 7, 0, opposite, right).wait_recv()
    ring(1, 7, 1, opposite, left).wait_recv()
    unpack_slot(0, opposite)
    unpack_slot(1, opposite)

    def group_copy(source, landing, send, recv, j, arriving):
        peer = lax.rem(me_g + j, GRP)
        origin = peer if arriving else me_g
        return pltpu.make_async_remote_copy(
            src_ref=source.at[pl.ds(pl.multiple_of(16 * peer, 16), 16)],
            dst_ref=landing.at[pl.ds(pl.multiple_of(16 * origin, 16), 16)],
            send_sem=send.at[peer], recv_sem=recv.at[origin],
            device_id=(me_s, peer), device_id_type=MESH,
        )

    def slab_copy(source, landing, send, recv, j, arriving):
        peer = lax.rem(me_s + j, SLAB)
        origin = peer if arriving else me_s
        return pltpu.make_async_remote_copy(
            src_ref=source.at[peer], dst_ref=landing.at[origin],
            send_sem=send.at[peer], recv_sem=recv.at[origin],
            device_id=(peer, me_g), device_id_type=MESH,
        )

    def reduce_copy(buffer, send, recv, j, arriving, along_group):
        size = GRP if along_group else SLAB
        mine = me_g if along_group else me_s
        peer = lax.rem(mine + j, size)
        origin = peer if arriving else mine
        return pltpu.make_async_remote_copy(
            src_ref=buffer.at[origin], dst_ref=buffer.at[origin],
            send_sem=send.at[peer], recv_sem=recv.at[origin],
            device_id=(me_s, peer) if along_group else (peer, me_g), device_id_type=MESH,
        )

    @pl.loop(1, GRP)
    def _(j):
        group_copy(early_out, early1, e1s, e1r, j, False).start()

    mine = pl.ds(pl.multiple_of(16 * me_g, 16), 16)
    early1[mine, :] = early_out[mine, :]

    @pl.loop(0, TILES)
    def _(t):
        lanes = pl.ds(pl.multiple_of(t * 128, 128), 128)
        rows = []
        for part in range(2):
            rows.append(
                jnp.concatenate(
                    [store[h, ids_ref[k, 2 * t + part]] for h in range(2) for k in range(SLOTS)], axis=1
                )
            )
        both = jnp.dot(jnp.concatenate(rows, axis=0), tiles[t], preferred_element_type=F32)
        lane = iota((ROWS, 128), 1)
        modelled = jnp.where(lane < 64, both[:ROWS], both[ROWS:])
        weight = conf_ref[:, lanes]
        residual = meas_ref[:, lanes] - modelled[24:27]
        sens[:, lanes] = modelled[:24]
        resid[0:3, lanes] = residual
        upper, lower = split_two(modelled[:24])
        norm_l[0:24, lanes] = upper
        norm_l[24:48, lanes] = lower
        weighted = [split_two(modelled[8 * c:8 * c + 8] * weight) for c in range(COMPS)]
        right_side = split_two(residual * weight)
        for part in range(2):
            for c in range(COMPS):
                start = 64 * part + 16 * c
                norm_r[start:start + 8, lanes] = weighted[c][part]
                norm_r[start + 8:start + 9, lanes] = right_side[part][c:c + 1]

    gram = lax.dot_general(
        norm_l[...].astype(BF16), norm_r[...].astype(BF16), (((1,), (1,)), ((), ())), preferred_element_type=F32
    )
    gram = gram[:24] + gram[24:]
    gram = gram + pltpu.roll(gram, 64, 1)
    normal = gram[:8] + pltpu.roll(gram[8:16], 112, 1) + pltpu.roll(gram[16:24], 96, 1)
    sub, lane = iota((8, 128), 0), iota((8, 128), 1)
    normal = jnp.where(lane < 16, normal, 0.0)
    for shift in (16, 32, 64):
        normal = normal + pltpu.roll(normal, shift, 1)
    own_chunk = (lane >> 4) == sub
    red1[me_g] = jnp.sum(jnp.where(own_chunk, normal, 0.0), axis=0, keepdims=True)

    @pl.loop(1, GRP)
    def _(j):
        reduce_copy(red1, r1s, r1r, j, False, True).start()

    @pl.loop(1, GRP)
    def _(j):
        group_copy(early_out, early1, e1s, e1r, j, True).wait_recv()

    def turn(landing, outgoing, comps):
        for c in range(comps):
            for upper_part in range(4):
                for side in range(2):
                    block = landing[pl.ds(128 * side + 4 * c + upper_part, 8, stride=16), :]
                    start = 64 * upper_part + 8 * (4 * side + c)
                    flip[start:start + 8, :] = swap_chunks(block)
        for upper_part in range(4):
            for lower_part in range(8):
                outgoing[8 * upper_part + lower_part] = flip[pl.ds(64 * upper_part + lower_part, 8, stride=8), :]

    turn(early1, early2_out, 4)

    @pl.loop(1, GRP)
    def _(j):
        reduce_copy(red1, r1s, r1r, j, True, True).wait_recv()

    red2[me_s] = jnp.sum(red1[...], axis=0)

    @pl.loop(1, SLAB)
    def _(j):
        reduce_copy(red2, r2s, r2r, j, False, False).start()

    @pl.loop(1, SLAB)
    def _(j):
        slab_copy(early2_out, early2, e2s, e2r, j, False).start()

    early2[me_s] = early2_out[me_s]

    @pl.loop(1, SLAB)
    def _(j):
        reduce_copy(red2, r2s, r2r, j, True, False).wait_recv()

    system = jnp.where(own_chunk, jnp.sum(red2[...], axis=0), 0.0)
    for shift in (16, 32, 64):
        system = system + pltpu.roll(system, shift, 1)
    column = lane & 15
    system = jnp.where(column == sub, system * (1.0 + DAMPING), system)
    for i in range(PARAMS):
        factor = system[:, i:i + 1]
        pivot_row = system[i:i + 1, :] / system[i:i + 1, i:i + 1]
        system = jnp.where(sub == i, pivot_row, system - factor * pivot_row)
    update = system[:, 8:9]
    flat = jnp.sum(jnp.where(lane == sub, update, 0.0), axis=0, keepdims=True)
    upd_ref[...] = flat[:, :PARAMS]

    for q in range(8):
        lanes = slice(512 * q, 512 * (q + 1))
        mask = scatter_m[:, lanes].astype(F32)
        for c in range(COMPS):
            predicted = jnp.sum(sens[8 * c:8 * c + 8, lanes] * update, axis=0, keepdims=True)
            remaining = split_two(resid[c:c + 1, lanes] - predicted)
            for part in range(2):
                start = HIGH * (3 * part + c)
                scatter_a[start:start + HIGH, lanes] = (mask * remaining[part]).astype(BF16)
    placed = jnp.dot(scatter_a[...], scatter_b[...], preferred_element_type=F32)
    placed = placed[:3 * HIGH] + placed[3 * HIGH:]
    for c in range(COMPS):
        for g in range(GRP):
            late_out[16 * g + 4 * c:16 * g + 4 * c + 4, :] = placed[HIGH * c + 4 * g:HIGH * c + 4 * g + 4, :]

    @pl.loop(1, GRP)
    def _(j):
        group_copy(late_out, late1, d1s, d1r, j, False).start()

    late1[mine, :] = late_out[mine, :]

    @pl.loop(1, GRP)
    def _(j):
        group_copy(late_out, late1, d1s, d1r, j, True).wait_recv()

    turn(late1, late2_out, 3)

    @pl.loop(1, SLAB)
    def _(j):
        slab_copy(late2_out, late2, d2s, d2r, j, False).start()

    late2[me_s] = late2_out[me_s]

    @pl.loop(1, SLAB)
    def _(j):
        slab_copy(early2_out, early2, e2s, e2r, j, True).wait_recv()

    @pl.loop(1, SLAB)
    def _(j):
        slab_copy(late2_out, late2, d2s, d2r, j, True).wait_recv()

    for first in range(0, SLAB, 8):
        for side in range(2):
            def rows_of(ref, c):
                return jnp.concatenate([ref[first + n, 4 * side + c:4 * side + c + 1, :] for n in range(8)], axis=0)

            confidence = rows_of(early2, 3)
            squares = jnp.zeros_like(confidence)
            results = []
            late_rows = [rows_of(late2, c) for c in range(COMPS)]
            for c in range(COMPS):
                results.append(rows_of(early2, c) - late_rows[c])
            for c in range(COMPS):
                results.append(confidence * late_rows[c])
                squares = squares + late_rows[c] * late_rows[c]
            results.append(confidence)
            results.append(confidence * squares)
            for r in range(8):
                flip[8 * r:8 * r + 8, :] = results[r]
            for n in range(8):
                start = 256 * (first + n) + 128 * side
                out_ref[:, start:start + 128] = flip[pl.ds(n, 8, stride=8), :]

    @pl.loop(0, CHUNKS)
    def _(j):
        i, h = j // 2, j % 2
        back, ahead = lax.rem(me_g + GRP - i, GRP), lax.rem(me_g + i, GRP)

        @pl.when((i < 7) | (h == 0))
        def _():
            ring(0, i, h, back, right).wait_send()

        @pl.when((i < 7) | (h == 1))
        def _():
            ring(1, i, h, ahead, left).wait_send()

    @pl.loop(1, GRP)
    def _(j):
        group_copy(early_out, early1, e1s, e1r, j, False).wait_send()
        group_copy(late_out, late1, d1s, d1r, j, False).wait_send()
        reduce_copy(red1, r1s, r1r, j, False, True).wait_send()

    @pl.loop(1, SLAB)
    def _(j):
        slab_copy(early2_out, early2, e2s, e2r, j, False).wait_send()
        slab_copy(late2_out, late2, d2s, d2r, j, False).wait_send()
        reduce_copy(red2, r2s, r2r, j, False, False).wait_send()


def body(fields, spline, measured, confidence, block_ids, live, owners):
    vmem = pl.BlockSpec(memory_space=pltpu.VMEM)
    smem = pl.BlockSpec(memory_space=pltpu.SMEM)
    dma = pltpu.SemaphoreType.DMA
    received, update = pl.pallas_call(
        kernel,
        out_shape=(
            jax.ShapeDtypeStruct((8, PEERS * CAP), F32),
            jax.ShapeDtypeStruct((1, PARAMS), F32),
        ),
        in_specs=[smem, smem, vmem, pl.BlockSpec(memory_space=pl.ANY), vmem, vmem, vmem],
        out_specs=(vmem, vmem),
        scratch_shapes=[
            pltpu.VMEM((3, 8, SLOTS, SUBSETS), BF16),
            dma,
            pltpu.VMEM((2, GRP, PACKED, HALF), BF16),
            pltpu.VMEM((2, GRP * BLOCKS, ROWS, HALF), BF16),
            pltpu.VMEM((TILES, SLOTS * BLK, 128), BF16),
            pltpu.VMEM((3, 32, 128), F32),
            pltpu.VMEM((PEERS, 128), F32),
            pltpu.VMEM((CHUNK, CHUNK + 128), BF16),
            pltpu.VMEM((BLOCKS * ROWS, PACKED), BF16),
            pltpu.VMEM((SUBSETS, 128), BF16),
            pltpu.VMEM((HIGH, SUBSETS), BF16),
            pltpu.VMEM((6 * HIGH, SUBSETS), BF16),
            pltpu.VMEM((8 * HIGH, 128), F32),
            pltpu.VMEM((24, SUBSETS), F32),
            pltpu.VMEM((8, SUBSETS), F32),
            pltpu.VMEM((48, SUBSETS), F32),
            pltpu.VMEM((128, SUBSETS), F32),
            pltpu.VMEM((GRP, 1, 128), F32),
            pltpu.VMEM((SLAB, 1, 128), F32),
            pltpu.VMEM((GRP * 16, 128), F32),
            pltpu.VMEM((GRP * 16, 128), F32),
            pltpu.VMEM((SLAB, 8, 128), F32),
            pltpu.VMEM((SLAB, 8, 128), F32),
            pltpu.VMEM((GRP * 16, 128), F32),
            pltpu.VMEM((GRP * 16, 128), F32),
            pltpu.VMEM((SLAB, 8, 128), F32),
            pltpu.VMEM((SLAB, 8, 128), F32),
            pltpu.VMEM((256, 128), F32),
            dma((2, 8, 2)), dma((2, 8, 2)),
            dma((GRP,)), dma((GRP,)), dma((SLAB,)), dma((SLAB,)),
            dma((GRP,)), dma((GRP,)), dma((SLAB,)), dma((SLAB,)),
            dma((GRP,)), dma((GRP,)), dma((SLAB,)), dma((SLAB,)),
        ],
        compiler_params=pltpu.CompilerParams(
            collective_id=0, has_side_effects=True, vmem_limit_bytes=56 * 1024 * 1024
        ),
    )(
        block_ids.T, live, fields, spline, measured,
        confidence.reshape(1, SUBSETS), owners.reshape(1, SUBSETS),
    )
    return (received, update.reshape(PARAMS))


def solution(mesh):
    placed = (
        P(None, ("slab", "grp")),
        P(None, None, None, ("slab", "grp")),
        P(None, ("slab", "grp")),
        P(("slab", "grp")),
        P(("slab", "grp"), None),
        P(("slab", "grp")),
        P(("slab", "grp"), None),
    )
    return jax.shard_map(
        body, mesh=mesh, in_specs=placed, out_specs=(P(None, ("slab", "grp")), P()), check_vma=False
    )
```

```python
import functools

import jax
import jax.numpy as jnp
from jax import lax
from jax.experimental import pallas as pl
from jax.experimental.pallas import tpu as pltpu
from jax.sharding import PartitionSpec as P

MESH = pl.DeviceIdType.MESH
F32 = jnp.float32
BF16 = jnp.bfloat16
DAMPING = 0.05

PARAMS = 8
COMPS = 3
CHANNELS = 27
ROWS = 32
BLOCKS = 4
PACKED = 112
BLK = 512
PIECE = 128
PIECES = 4
EXPRESS = 3
STEPS = 7
SLOTS = 4
CAP = 16
GRP = 16
SLAB = 32
SUBSETS = 4096
TILES = 32
CHUNK = 256
CHUNKS = 16
PEERS = 512
HIGH = 64


def iota(shape, axis):
    return lax.broadcasted_iota(jnp.int32, shape, axis)


def split_two(value):
    upper = value.astype(BF16).astype(F32)
    return upper, (value - upper).astype(BF16).astype(F32)


def swap_chunks(value):
    sub, lane = iota((8, 128), 0), iota((8, 128), 1)
    for bit in range(3):
        step = 1 << bit
        sub_bit, lane_bit = (sub >> bit) & 1, (lane >> (4 + bit)) & 1
        upward = pltpu.roll(pltpu.roll(value, 16 * step, 1), 8 - step, 0)
        downward = pltpu.roll(pltpu.roll(value, 128 - 16 * step, 1), step, 0)
        value = jnp.where(sub_bit == lane_bit, value, jnp.where(sub_bit == 0, upward, downward))
    return value


def kernel(
    ids_ref, live_ref, fields_ref, spline_hbm, meas_ref, conf_ref, own_ref,
    out_ref, upd_ref,
    spline_ref, spline_sem, land, store, tiles, sp32, carry, upper_ref, unpack_ref,
    scatter_b, scatter_m, scatter_a, early_acc, first_half, sens, resid, norm_l, norm_r,
    red1, red2, early_out, early1, early2_out, early2, late_out, late1, late2_out, late2, flip,
    ag_send, ag_recv, r1s, r1r, r2s, r2r, e1s, e1r, e2s, e2r, d1s, d1r, d2s, d2r,
):
    me_s = lax.axis_index("slab")
    me_g = lax.axis_index("grp")

    barrier = pltpu.get_barrier_semaphore()

    for j in (1, EXPRESS, GRP - EXPRESS, GRP - 1):
        pl.semaphore_signal(barrier, inc=1, device_id=(me_s, lax.rem(me_g + j, GRP)), device_id_type=MESH)

    @pl.loop(1, SLAB)
    def _(j):
        pl.semaphore_signal(barrier, inc=1, device_id=(lax.rem(me_s + j, SLAB), me_g), device_id_type=MESH)

    spline_copy = pltpu.make_async_copy(spline_hbm, spline_ref, spline_sem)
    spline_copy.start()

    row = iota((PACKED, CHANNELS), 0)
    channel = iota((PACKED, CHANNELS), 1)
    packed = None
    for j in range(BLOCKS):
        new = row - CHANNELS * j
        source = jnp.where(new < 24, 3 + 3 * (new & 7) + (new >> 3), new - 24)
        pick = (channel == source) & (new >= 0) & (new < CHANNELS)
        part = jnp.dot(
            jnp.where(pick, 1.0, 0.0).astype(BF16), fields_ref[:, j * BLK:(j + 1) * BLK], preferred_element_type=F32
        )
        packed = part if packed is None else packed + part
    packed = packed.astype(BF16)
    for p in range(PIECES):
        land[p, me_g] = packed[:, p * PIECE:(p + 1) * PIECE]

    def place_at(direction, distance):
        return lax.rem(me_g + (distance if direction == 0 else GRP - distance), GRP)

    def hop(direction, p, position, reach):
        slot = place_at(1 - direction, position)
        return pltpu.make_async_remote_copy(
            src_ref=land.at[p, slot], dst_ref=land.at[p, slot],
            send_sem=ag_send.at[direction, p, position + reach], recv_sem=ag_recv.at[direction, p, position + reach],
            device_id=(me_s, place_at(direction, reach)), device_id_type=MESH,
        )

    def landed(direction, p, position):
        slot = place_at(1 - direction, position)
        pltpu.make_async_remote_copy(
            src_ref=land.at[p, slot], dst_ref=land.at[p, slot],
            send_sem=ag_send.at[direction, p, position], recv_sem=ag_recv.at[direction, p, position],
            device_id=(me_s, place_at(direction, 1)), device_id_type=MESH,
        ).wait_recv()

    def unpack_slots(p, slots):
        joined = jnp.concatenate([land[p, slot] for slot in slots], axis=1)
        rows = jnp.dot(unpack_ref[...], joined, preferred_element_type=F32).astype(BF16)
        for n, slot in enumerate(slots):
            part = rows[:, n * PIECE:(n + 1) * PIECE].reshape(BLOCKS, ROWS, PIECE)
            store[p, pl.ds(BLOCKS * slot, BLOCKS)] = part

    def build_tile(t):
        lanes = pl.ds(pl.multiple_of(t * 128, 128), 128)
        for axis in range(3):
            part = spline_ref[axis, :, :, lanes].astype(F32)
            for e in range(8):
                sp32[axis, e * 4:(e + 1) * 4, :] = part[e]
        live_row = jnp.where(iota((8, 128), 1) < 64, live_ref[2 * t], live_ref[2 * t + 1])
        for k in range(SLOTS):
            along_z = sp32[0, pl.ds(k, 8, stride=4), :]
            along_y = sp32[1, pl.ds(k, 8, stride=4), :]
            along_x = sp32[2, pl.ds(k, 8, stride=4), :]
            along_z = jnp.where(live_row > k, along_z, 0.0)
            for z in range(8):
                face = along_z[z:z + 1, :] * along_y
                cells = (face[:, None, :] * along_x[None, :, :]).reshape(64, 128)
                start = (z // 2) * 512 + k * PIECE + (z % 2) * 64
                tiles[t, start:start + 64, :] = cells.astype(BF16)

    def place_chunk(j):
        lanes = pl.ds(pl.multiple_of(j * CHUNK, CHUNK), CHUNK)
        owner = own_ref[:, lanes]
        onehot = jnp.where(iota((PEERS, CHUNK), 0) == owner, 1.0, 0.0)
        counted = jnp.dot(onehot.astype(BF16), upper_ref[...], preferred_element_type=F32)
        before = carry[...]
        rank = jnp.sum(
            onehot * (counted[:, :CHUNK] + jnp.concatenate([before, before], axis=1)), axis=0, keepdims=True
        )
        carry[...] = before + counted[:, CHUNK:]
        low = ((owner >> 4) & 7) * CAP + rank.astype(jnp.int32)
        high = (owner & 15) * 4 + (owner >> 7)
        column = jnp.where(iota((128, CHUNK), 0) == low, 1.0, 0.0).T.astype(BF16)
        scatter_b[lanes, :] = column
        mask = jnp.where(iota((HIGH, CHUNK), 0) == high, 1.0, 0.0)
        scatter_m[:, lanes] = mask.astype(BF16)
        pieces = []
        for value in [meas_ref[c:c + 1, lanes] for c in range(COMPS)] + [conf_ref[:, lanes]]:
            pieces.append(split_two(value))
        stacked = jnp.concatenate(
            [(mask * pieces[c][part]).astype(BF16) for part in range(2) for c in range(4)], axis=0
        )
        early_acc[...] += jnp.dot(stacked, column, preferred_element_type=F32)

    pl.semaphore_wait(barrier, SLAB + 3)

    def forward(direction, p, position):
        if p % 2 == direction:
            hop(direction, p, position, 1).start()
        else:
            if isinstance(position, int) and position >= 7:
                return

            @pl.when(position < 7)
            def _():
                hop(direction, p, position, 1).start()

    first, second = (0, 1), (2, 3)
    both = (0, 1)

    for p in first:
        for direction in both:
            hop(direction, p, 0, EXPRESS).start()
            hop(direction, p, 0, 1).start()
    for p in second:
        for direction in both:
            hop(direction, p, 0, 1).start()

    row, col = iota((CHUNK, CHUNK + 128), 0), iota((CHUNK, CHUNK + 128), 1)
    upper_ref[...] = jnp.where((row < col) | (col >= CHUNK), 1.0, 0.0).astype(BF16)
    row, col = iota((BLOCKS * ROWS, PACKED), 0), iota((BLOCKS * ROWS, PACKED), 1)
    unpack = jnp.zeros((BLOCKS * ROWS, PACKED), F32)
    for j in range(BLOCKS):
        inside = (row >= ROWS * j) & (row < ROWS * j + CHANNELS)
        unpack = jnp.where(inside & (col == row - (ROWS - CHANNELS) * j), 1.0, unpack)
    unpack_ref[...] = unpack.astype(BF16)
    carry[...] = jnp.zeros_like(carry)
    early_acc[...] = jnp.zeros_like(early_acc)
    norm_r[...] = jnp.zeros_like(norm_r)

    spline_copy.wait()
    for p in range(PIECES):
        unpack_slots(p, [me_g])

    def build(lo, hi):
        @pl.loop(lo, hi)
        def _(j):
            build_tile(2 * j)
            build_tile(2 * j + 1)
            place_chunk(j)

    build(0, 2)

    def second_step(i):
        for p in second:
            for direction in both:
                landed(direction, p, i)
                forward(direction, p, i)

    def unpack_both(p, position):
        unpack_slots(p, [place_at(0, position), place_at(1, position)])

    @pl.loop(1, STEPS)
    def _(i):
        second_step(i)

        @pl.when(i == 1)
        def _():
            for p in first:
                for direction in both:
                    landed(direction, p, 1)
                    hop(direction, p, 1, 1).start()

        build(2 * i, 2 * i + 1)
        position = i + EXPRESS - 1

        for p in first:
            for direction in both:
                if p % 2 == direction:
                    landed(direction, p, position)

                    @pl.when(position < 8)
                    def _():
                        hop(direction, p, position, 1).start()
                else:
                    @pl.when(position < 8)
                    def _():
                        landed(direction, p, position)

                    @pl.when(position < 7)
                    def _():
                        hop(direction, p, position, 1).start()

        for p in second:
            unpack_both(p, i)

        build(2 * i + 1, 2 * i + 2)

        @pl.when(i == 2)
        def _():
            for p in first:
                for direction in both:
                    landed(direction, p, 2)

        @pl.when(i < 3)
        def _():
            for p in first:
                unpack_both(p, i)

        for p in first:
            unpack_both(p, position)

    build(2 * STEPS, CHUNKS)

    total = early_acc[0:4 * HIGH, :] + early_acc[4 * HIGH:, :]
    for c in range(4):
        for g in range(GRP):
            early_out[16 * g + 4 * c:16 * g + 4 * c + 4, :] = total[HIGH * c + 4 * g:HIGH * c + 4 * g + 4, :]

    def group_copy(source, landing, send, recv, j, arriving):
        peer = lax.rem(me_g + j, GRP)
        origin = peer if arriving else me_g
        flat = len(source.shape) == 2
        return pltpu.make_async_remote_copy(
            src_ref=source.at[pl.ds(pl.multiple_of(16 * peer, 16), 16)] if flat else source.at[peer],
            dst_ref=landing.at[pl.ds(pl.multiple_of(16 * origin, 16), 16)] if flat else landing.at[origin],
            send_sem=send.at[peer], recv_sem=recv.at[origin],
            device_id=(me_s, peer), device_id_type=MESH,
        )

    def slab_copy(source, landing, send, recv, j, arriving):
        peer = lax.rem(me_s + j, SLAB)
        origin = peer if arriving else me_s
        return pltpu.make_async_remote_copy(
            src_ref=source.at[peer], dst_ref=landing.at[origin],
            send_sem=send.at[peer], recv_sem=recv.at[origin],
            device_id=(peer, me_g), device_id_type=MESH,
        )

    def reduce_copy(buffer, send, recv, j, arriving, along_group):
        size = GRP if along_group else SLAB
        mine = me_g if along_group else me_s
        peer = lax.rem(mine + j, size)
        origin = peer if arriving else mine
        return pltpu.make_async_remote_copy(
            src_ref=buffer.at[origin], dst_ref=buffer.at[origin],
            send_sem=send.at[peer], recv_sem=recv.at[origin],
            device_id=(me_s, peer) if along_group else (peer, me_g), device_id_type=MESH,
        )

    def interpolate(t, half):
        rows = []
        for part in range(2):
            rows.append(
                jnp.concatenate(
                    [store[p, ids_ref[k, 2 * t + part]] for p in (2 * half, 2 * half + 1) for k in range(SLOTS)], axis=1
                )
            )
        both = jnp.dot(
            jnp.concatenate(rows, axis=0), tiles[t, 1024 * half:1024 * half + 1024], preferred_element_type=F32
        )
        return jnp.where(iota((ROWS, 128), 1) < 64, both[:ROWS], both[ROWS:])

    def interpolate_first(lo, hi):
        @pl.loop(lo, hi, unroll=2)
        def _(t):
            first_half[:, pl.ds(pl.multiple_of(t * 128, 128), 128)] = interpolate(t, 0)

    interpolate_first(0, 8)
    second_step(STEPS)
    interpolate_first(8, TILES)
    for p in second:
        unpack_both(p, STEPS)
        landed(p % 2, p, STEPS + 1)
        unpack_slots(p, [place_at(0, STEPS + 1)])

    @pl.loop(0, TILES, unroll=2)
    def _(t):
        lanes = pl.ds(pl.multiple_of(t * 128, 128), 128)
        modelled = first_half[:, lanes] + interpolate(t, 1)
        weight = conf_ref[:, lanes]
        residual = meas_ref[:, lanes] - modelled[24:27]
        sens[:, lanes] = modelled[:24]
        resid[0:3, lanes] = residual
        upper, lower = split_two(modelled[:24])
        norm_l[0:24, lanes] = upper
        norm_l[24:48, lanes] = lower
        weighted = [split_two(modelled[8 * c:8 * c + 8] * weight) for c in range(COMPS)]
        right_side = split_two(residual * weight)
        for part in range(2):
            for c in range(COMPS):
                start = 64 * part + 16 * c
                norm_r[start:start + 8, lanes] = weighted[c][part]
                norm_r[start + 8:start + 9, lanes] = right_side[part][c:c + 1]

    gram = lax.dot_general(
        norm_l[...].astype(BF16), norm_r[...].astype(BF16), (((1,), (1,)), ((), ())), preferred_element_type=F32
    )
    gram = gram[:24] + gram[24:]
    gram = gram + pltpu.roll(gram, 64, 1)
    normal = gram[:8] + pltpu.roll(gram[8:16], 112, 1) + pltpu.roll(gram[16:24], 96, 1)
    sub, lane = iota((8, 128), 0), iota((8, 128), 1)
    normal = jnp.where(lane < 16, normal, 0.0)
    for shift in (16, 32, 64):
        normal = normal + pltpu.roll(normal, shift, 1)
    own_chunk = (lane >> 4) == sub
    red1[me_g] = jnp.sum(jnp.where(own_chunk, normal, 0.0), axis=0, keepdims=True)

    @pl.loop(1, GRP)
    def _(j):
        reduce_copy(red1, r1s, r1r, j, False, True).start()

    def turn(landing, outgoing, comps):
        for c in range(comps):
            for upper_part in range(4):
                for side in range(2):
                    if len(landing.shape) == 2:
                        block = landing[pl.ds(128 * side + 4 * c + upper_part, 8, stride=16), :]
                    else:
                        block = landing[8 * side:8 * side + 8, c, upper_part, :]
                    start = 64 * upper_part + 8 * (4 * side + c)
                    flip[start:start + 8, :] = swap_chunks(block)
        for upper_part in range(4):
            for lower_part in range(8):
                outgoing[8 * upper_part + lower_part] = flip[pl.ds(64 * upper_part + lower_part, 8, stride=8), :]

    @pl.loop(1, GRP)
    def _(j):
        reduce_copy(red1, r1s, r1r, j, True, True).wait_recv()

    red2[me_s] = jnp.sum(red1[...], axis=0)

    @pl.loop(1, SLAB)
    def _(j):
        reduce_copy(red2, r2s, r2r, j, False, False).start()

    @pl.loop(1, GRP)
    def _(j):
        group_copy(early_out, early1, e1s, e1r, j, False).start()

    mine = pl.ds(pl.multiple_of(16 * me_g, 16), 16)
    early1[mine, :] = early_out[mine, :]

    @pl.loop(1, SLAB)
    def _(j):
        reduce_copy(red2, r2s, r2r, j, True, False).wait_recv()

    system = jnp.where(own_chunk, jnp.sum(red2[...], axis=0), 0.0)
    for shift in (16, 32, 64):
        system = system + pltpu.roll(system, shift, 1)
    column = lane & 15
    system = jnp.where(column == sub, system * (1.0 + DAMPING), system)
    for i in range(PARAMS):
        factor = system[:, i:i + 1]
        pivot_row = system[i:i + 1, :] / system[i:i + 1, i:i + 1]
        system = jnp.where(sub == i, pivot_row, system - factor * pivot_row)
    update = system[:, 8:9]
    flat = jnp.sum(jnp.where(lane == sub, update, 0.0), axis=0, keepdims=True)
    upd_ref[...] = flat[:, :PARAMS]

    for q in range(8):
        lanes = slice(512 * q, 512 * (q + 1))
        mask = scatter_m[:, lanes].astype(F32)
        for c in range(COMPS):
            predicted = jnp.sum(sens[8 * c:8 * c + 8, lanes] * update, axis=0, keepdims=True)
            remaining = split_two(resid[c:c + 1, lanes] - predicted)
            for part in range(2):
                start = HIGH * (3 * part + c)
                scatter_a[start:start + HIGH, lanes] = (mask * remaining[part]).astype(BF16)
    placed = jnp.dot(scatter_a[...], scatter_b[...], preferred_element_type=F32)
    placed = placed[:3 * HIGH] + placed[3 * HIGH:]
    for c in range(COMPS):
        for g in range(GRP):
            late_out[g, c] = placed[HIGH * c + 4 * g:HIGH * c + 4 * g + 4, :]

    @pl.loop(1, GRP)
    def _(j):
        group_copy(late_out, late1, d1s, d1r, j, False).start()

    late1[me_g] = late_out[me_g]

    @pl.loop(1, GRP)
    def _(j):
        group_copy(early_out, early1, e1s, e1r, j, True).wait_recv()

    turn(early1, early2_out, 4)

    @pl.loop(1, SLAB)
    def _(j):
        slab_copy(early2_out, early2, e2s, e2r, j, False).start()

    early2[me_s] = early2_out[me_s]

    @pl.loop(1, GRP)
    def _(j):
        group_copy(late_out, late1, d1s, d1r, j, True).wait_recv()

    turn(late1, late2_out, 3)

    @pl.loop(1, SLAB)
    def _(j):
        slab_copy(late2_out, late2, d2s, d2r, j, False).start()

    late2[me_s] = late2_out[me_s]

    @pl.loop(1, SLAB)
    def _(j):
        slab_copy(early2_out, early2, e2s, e2r, j, True).wait_recv()

    @pl.loop(1, SLAB)
    def _(j):
        slab_copy(late2_out, late2, d2s, d2r, j, True).wait_recv()

    for first in range(0, SLAB, 8):
        for side in range(2):
            def rows_of(ref, c):
                return jnp.concatenate([ref[first + n, 4 * side + c:4 * side + c + 1, :] for n in range(8)], axis=0)

            confidence = rows_of(early2, 3)
            squares = jnp.zeros_like(confidence)
            results = []
            late_rows = [rows_of(late2, c) for c in range(COMPS)]
            for c in range(COMPS):
                results.append(rows_of(early2, c) - late_rows[c])
            for c in range(COMPS):
                results.append(confidence * late_rows[c])
                squares = squares + late_rows[c] * late_rows[c]
            results.append(confidence)
            results.append(confidence * squares)
            for r in range(8):
                flip[8 * r:8 * r + 8, :] = results[r]
            for n in range(8):
                start = 256 * (first + n) + 128 * side
                out_ref[:, start:start + 128] = flip[pl.ds(n, 8, stride=8), :]

    for p in range(PIECES):
        for direction in both:
            @pl.loop(1, 9 if p % 2 == direction else 8)
            def _(position):
                hop(direction, p, position - 1, 1).wait_send()

    @pl.loop(1, GRP)
    def _(j):
        group_copy(early_out, early1, e1s, e1r, j, False).wait_send()
        group_copy(late_out, late1, d1s, d1r, j, False).wait_send()
        reduce_copy(red1, r1s, r1r, j, False, True).wait_send()

    @pl.loop(1, SLAB)
    def _(j):
        slab_copy(early2_out, early2, e2s, e2r, j, False).wait_send()
        slab_copy(late2_out, late2, d2s, d2r, j, False).wait_send()
        reduce_copy(red2, r2s, r2r, j, False, False).wait_send()


def body(fields, spline, measured, confidence, block_ids, live, owners):
    vmem = pl.BlockSpec(memory_space=pltpu.VMEM)
    smem = pl.BlockSpec(memory_space=pltpu.SMEM)
    dma = pltpu.SemaphoreType.DMA
    received, update = pl.pallas_call(
        kernel,
        out_shape=(
            jax.ShapeDtypeStruct((8, PEERS * CAP), F32),
            jax.ShapeDtypeStruct((1, PARAMS), F32),
        ),
        in_specs=[smem, smem, vmem, pl.BlockSpec(memory_space=pl.ANY), vmem, vmem, vmem],
        out_specs=(vmem, vmem),
        scratch_shapes=[
            pltpu.VMEM((3, 8, SLOTS, SUBSETS), BF16),
            dma,
            pltpu.VMEM((PIECES, GRP, PACKED, PIECE), BF16),
            pltpu.VMEM((PIECES, GRP * BLOCKS, ROWS, PIECE), BF16),
            pltpu.VMEM((TILES, SLOTS * BLK, 128), BF16),
            pltpu.VMEM((3, 32, 128), F32),
            pltpu.VMEM((PEERS, 128), F32),
            pltpu.VMEM((CHUNK, CHUNK + 128), BF16),
            pltpu.VMEM((BLOCKS * ROWS, PACKED), BF16),
            pltpu.VMEM((SUBSETS, 128), BF16),
            pltpu.VMEM((HIGH, SUBSETS), BF16),
            pltpu.VMEM((6 * HIGH, SUBSETS), BF16),
            pltpu.VMEM((8 * HIGH, 128), F32),
            pltpu.VMEM((ROWS, SUBSETS), F32),
            pltpu.VMEM((24, SUBSETS), F32),
            pltpu.VMEM((8, SUBSETS), F32),
            pltpu.VMEM((48, SUBSETS), F32),
            pltpu.VMEM((128, SUBSETS), F32),
            pltpu.VMEM((GRP, 1, 128), F32),
            pltpu.VMEM((SLAB, 1, 128), F32),
            pltpu.VMEM((GRP * 16, 128), F32),
            pltpu.VMEM((GRP * 16, 128), F32),
            pltpu.VMEM((SLAB, 8, 128), F32),
            pltpu.VMEM((SLAB, 8, 128), F32),
            pltpu.VMEM((GRP, COMPS, 4, 128), F32),
            pltpu.VMEM((GRP, COMPS, 4, 128), F32),
            pltpu.VMEM((SLAB, 8, 128), F32),
            pltpu.VMEM((SLAB, 8, 128), F32),
            pltpu.VMEM((256, 128), F32),
            dma((2, PIECES, 9)), dma((2, PIECES, 9)),
            dma((GRP,)), dma((GRP,)), dma((SLAB,)), dma((SLAB,)),
            dma((GRP,)), dma((GRP,)), dma((SLAB,)), dma((SLAB,)),
            dma((GRP,)), dma((GRP,)), dma((SLAB,)), dma((SLAB,)),
        ],
        compiler_params=pltpu.CompilerParams(
            collective_id=0, has_side_effects=True, vmem_limit_bytes=56 * 1024 * 1024
        ),
    )(
        block_ids.T, live, fields, spline, measured,
        confidence.reshape(1, SUBSETS), owners.reshape(1, SUBSETS),
    )
    return (received, update.reshape(PARAMS))


def solution(mesh):
    placed = (
        P(None, ("slab", "grp")),
        P(None, None, None, ("slab", "grp")),
        P(None, ("slab", "grp")),
        P(("slab", "grp")),
        P(("slab", "grp"), None),
        P(("slab", "grp")),
        P(("slab", "grp"), None),
    )
    return jax.shard_map(
        body, mesh=mesh, in_specs=placed, out_specs=(P(None, ("slab", "grp")), P()), check_vma=False
    )
```

```python
import functools

import jax
import jax.numpy as jnp
from jax import lax
from jax.experimental import pallas as pl
from jax.experimental.pallas import tpu as pltpu
from jax.sharding import PartitionSpec as P

MESH = pl.DeviceIdType.MESH
F32 = jnp.float32
BF16 = jnp.bfloat16
DAMPING = 0.05

PARAMS = 8
COMPS = 3
CHANNELS = 27
ROWS = 32
BLOCKS = 4
PACKED = 112
BLK = 512
PIECE = 128
PIECES = 4
STEPS = 6
SLOTS = 4
CAP = 16
GRP = 16
SLAB = 32
SUBSETS = 4096
TILES = 32
CHUNK = 256
CHUNKS = 16
PEERS = 512
HIGH = 64


def iota(shape, axis):
    return lax.broadcasted_iota(jnp.int32, shape, axis)


def split_two(value):
    upper = value.astype(BF16).astype(F32)
    return upper, (value - upper).astype(BF16).astype(F32)


def swap_chunks(value):
    sub, lane = iota((8, 128), 0), iota((8, 128), 1)
    for bit in range(3):
        step = 1 << bit
        sub_bit, lane_bit = (sub >> bit) & 1, (lane >> (4 + bit)) & 1
        upward = pltpu.roll(pltpu.roll(value, 16 * step, 1), 8 - step, 0)
        downward = pltpu.roll(pltpu.roll(value, 128 - 16 * step, 1), step, 0)
        value = jnp.where(sub_bit == lane_bit, value, jnp.where(sub_bit == 0, upward, downward))
    return value


def kernel(
    ids_ref, live_ref, fields_ref, spline_hbm, meas_ref, conf_ref, own_ref,
    out_ref, upd_ref,
    spline_ref, spline_sem, land, store, tiles, sp32, carry, upper_ref, unpack_ref,
    scatter_b, scatter_m, early_acc, first_half, sens, resid, norm_l, norm_r,
    red1, red2, early_out, early1, early2_out, early2, late_out, late1, late2_out, late2, flip,
    ag_send, ag_recv, r1s, r1r, r2s, r2r, e1s, e1r, e2s, e2r, d1s, d1r, d2s, d2r,
):
    me_s = lax.axis_index("slab")
    me_g = lax.axis_index("grp")

    barrier = pltpu.get_barrier_semaphore()

    for j in (1, 2, GRP - 2, GRP - 1):
        pl.semaphore_signal(barrier, inc=1, device_id=(me_s, lax.rem(me_g + j, GRP)), device_id_type=MESH)

    @pl.loop(1, SLAB)
    def _(j):
        pl.semaphore_signal(barrier, inc=1, device_id=(lax.rem(me_s + j, SLAB), me_g), device_id_type=MESH)

    spline_copy = pltpu.make_async_copy(spline_hbm, spline_ref, spline_sem)
    spline_copy.start()

    row = iota((PACKED, CHANNELS), 0)
    channel = iota((PACKED, CHANNELS), 1)
    packed = None
    for j in range(BLOCKS):
        new = row - CHANNELS * j
        source = jnp.where(new < 24, 3 + 3 * (new & 7) + (new >> 3), new - 24)
        pick = (channel == source) & (new >= 0) & (new < CHANNELS)
        part = jnp.dot(
            jnp.where(pick, 1.0, 0.0).astype(BF16), fields_ref[:, j * BLK:(j + 1) * BLK], preferred_element_type=F32
        )
        packed = part if packed is None else packed + part
    packed = packed.astype(BF16)
    for p in range(PIECES):
        land[p, me_g] = packed[:, p * PIECE:(p + 1) * PIECE]

    def place_at(direction, distance):
        return lax.rem(me_g + (distance if direction == 0 else GRP - distance), GRP)

    def hop(direction, p, position, reach):
        slot = place_at(1 - direction, position)
        return pltpu.make_async_remote_copy(
            src_ref=land.at[p, slot], dst_ref=land.at[p, slot],
            send_sem=ag_send.at[direction, p, position + reach], recv_sem=ag_recv.at[direction, p, position + reach],
            device_id=(me_s, place_at(direction, reach)), device_id_type=MESH,
        )

    def landed(direction, p, position):
        slot = place_at(1 - direction, position)
        pltpu.make_async_remote_copy(
            src_ref=land.at[p, slot], dst_ref=land.at[p, slot],
            send_sem=ag_send.at[direction, p, position], recv_sem=ag_recv.at[direction, p, position],
            device_id=(me_s, place_at(direction, 1)), device_id_type=MESH,
        ).wait_recv()

    def unpack_slots(p, slots):
        joined = jnp.concatenate([land[p, slot] for slot in slots], axis=1)
        rows = jnp.dot(unpack_ref[...], joined, preferred_element_type=F32).astype(BF16)
        for n, slot in enumerate(slots):
            part = rows[:, n * PIECE:(n + 1) * PIECE].reshape(BLOCKS, ROWS, PIECE)
            store[p, pl.ds(BLOCKS * slot, BLOCKS)] = part

    def build_tile(t):
        lanes = pl.ds(pl.multiple_of(t * 128, 128), 128)
        for axis in range(3):
            part = spline_ref[axis, :, :, lanes].astype(F32)
            for e in range(8):
                sp32[axis, e * 4:(e + 1) * 4, :] = part[e]
        live_row = jnp.where(iota((8, 128), 1) < 64, live_ref[2 * t], live_ref[2 * t + 1])
        for k in range(SLOTS):
            along_z = sp32[0, pl.ds(k, 8, stride=4), :]
            along_y = sp32[1, pl.ds(k, 8, stride=4), :]
            along_x = sp32[2, pl.ds(k, 8, stride=4), :]
            along_z = jnp.where(live_row > k, along_z, 0.0)
            for z in range(8):
                face = along_z[z:z + 1, :] * along_y
                cells = (face[:, None, :] * along_x[None, :, :]).reshape(64, 128)
                start = (z // 2) * 512 + k * PIECE + (z % 2) * 64
                tiles[t, start:start + 64, :] = cells.astype(BF16)

    def place_chunk(j):
        lanes = pl.ds(pl.multiple_of(j * CHUNK, CHUNK), CHUNK)
        owner = own_ref[:, lanes]
        onehot = jnp.where(iota((PEERS, CHUNK), 0) == owner, 1.0, 0.0)
        counted = jnp.dot(onehot.astype(BF16), upper_ref[...], preferred_element_type=F32)
        before = carry[...]
        rank = jnp.sum(
            onehot * (counted[:, :CHUNK] + jnp.concatenate([before, before], axis=1)), axis=0, keepdims=True
        )
        carry[...] = before + counted[:, CHUNK:]
        low = ((owner >> 4) & 7) * CAP + rank.astype(jnp.int32)
        high = (owner & 15) * 4 + (owner >> 7)
        column = jnp.where(iota((128, CHUNK), 0) == low, 1.0, 0.0).T.astype(BF16)
        scatter_b[lanes, :] = column
        mask = jnp.where(iota((HIGH, CHUNK), 0) == high, 1.0, 0.0).astype(BF16)
        scatter_m[:, lanes] = mask
        pieces = []
        for value in [meas_ref[c:c + 1, lanes] for c in range(COMPS)] + [conf_ref[:, lanes]]:
            pieces.append(split_two(value))
        stacked = jnp.concatenate(
            [mask * pieces[c][part].astype(BF16) for part in range(2) for c in range(4)], axis=0
        )
        early_acc[...] += jnp.dot(stacked, column, preferred_element_type=F32)

    pl.semaphore_wait(barrier, SLAB + 3)

    both = (0, 1)

    def send_step(p, step, position):
        for direction in both:
            @pl.when((step < STEPS - 1) | (p % 2 == direction))
            def _():
                hop(direction, p, position, 1 + (step % 3) // 2).start()

            @pl.when(step % 3 == 2)
            def _():
                hop(direction, p, position, 1).start()

    for p in range(PIECES):
        for direction in both:
            hop(direction, p, 0, 1).start()

    row, col = iota((CHUNK, CHUNK + 128), 0), iota((CHUNK, CHUNK + 128), 1)
    upper_ref[...] = jnp.where((row < col) | (col >= CHUNK), 1.0, 0.0).astype(BF16)
    row, col = iota((BLOCKS * ROWS, PACKED), 0), iota((BLOCKS * ROWS, PACKED), 1)
    unpack = jnp.zeros((BLOCKS * ROWS, PACKED), F32)
    for j in range(BLOCKS):
        inside = (row >= ROWS * j) & (row < ROWS * j + CHANNELS)
        unpack = jnp.where(inside & (col == row - (ROWS - CHANNELS) * j), 1.0, unpack)
    unpack_ref[...] = unpack.astype(BF16)
    carry[...] = jnp.zeros_like(carry)
    early_acc[...] = jnp.zeros_like(early_acc)
    norm_r[...] = jnp.zeros_like(norm_r)

    def build(lo, hi):
        @pl.loop(lo, hi)
        def _(j):
            build_tile(2 * j)
            build_tile(2 * j + 1)
            place_chunk(j)

    def unpack_both(p, position):
        unpack_slots(p, [place_at(0, position), place_at(1, position)])

    spline_copy.wait()
    for p in range(PIECES):
        unpack_slots(p, [me_g])
    build(0, 2)

    @pl.loop(1, STEPS)
    def _(step):
        position = step + step // 3
        for group in range(2):
            pieces = (2 * group, 2 * group + 1)
            for p in pieces:
                for direction in both:
                    landed(direction, p, position)
                send_step(p, step, position)
            for p in pieces:
                unpack_both(p, position)

            @pl.when(step == 3)
            def _():
                for p in pieces:
                    for direction in both:
                        landed(direction, p, 3)
                    unpack_both(p, 3)

            turn_index = 2 * (step - 1) + group
            build(2 + (turn_index * 7) // 5, 2 + ((turn_index + 1) * 7) // 5)

    total = early_acc[0:4 * HIGH, :] + early_acc[4 * HIGH:, :]
    for c in range(4):
        for g in range(GRP):
            early_out[16 * g + 4 * c:16 * g + 4 * c + 4, :] = total[HIGH * c + 4 * g:HIGH * c + 4 * g + 4, :]

    def group_copy(source, landing, send, recv, j, arriving):
        peer = lax.rem(me_g + j, GRP)
        origin = peer if arriving else me_g
        flat = len(source.shape) == 2
        return pltpu.make_async_remote_copy(
            src_ref=source.at[pl.ds(pl.multiple_of(16 * peer, 16), 16)] if flat else source.at[peer],
            dst_ref=landing.at[pl.ds(pl.multiple_of(16 * origin, 16), 16)] if flat else landing.at[origin],
            send_sem=send.at[peer], recv_sem=recv.at[origin],
            device_id=(me_s, peer), device_id_type=MESH,
        )

    def slab_copy(source, landing, send, recv, j, arriving):
        peer = lax.rem(me_s + j, SLAB)
        origin = peer if arriving else me_s
        return pltpu.make_async_remote_copy(
            src_ref=source.at[pl.ds(pl.multiple_of(8 * peer, 8), 8)],
            dst_ref=landing.at[pl.ds(pl.multiple_of(8 * origin, 8), 8)],
            send_sem=send.at[peer], recv_sem=recv.at[origin],
            device_id=(peer, me_g), device_id_type=MESH,
        )

    def reduce_copy(buffer, send, recv, j, arriving, along_group):
        size = GRP if along_group else SLAB
        mine = me_g if along_group else me_s
        peer = lax.rem(mine + j, size)
        origin = peer if arriving else mine
        return pltpu.make_async_remote_copy(
            src_ref=buffer.at[origin], dst_ref=buffer.at[origin],
            send_sem=send.at[peer], recv_sem=recv.at[origin],
            device_id=(me_s, peer) if along_group else (peer, me_g), device_id_type=MESH,
        )

    def interpolate(t, half):
        rows = []
        for part in range(2):
            rows.append(
                jnp.concatenate(
                    [store[p, ids_ref[k, 2 * t + part]] for p in (2 * half, 2 * half + 1) for k in range(SLOTS)], axis=1
                )
            )
        both = jnp.dot(
            jnp.concatenate(rows, axis=0), tiles[t, 1024 * half:1024 * half + 1024], preferred_element_type=F32
        )
        return jnp.where(iota((ROWS, 128), 1) < 64, both[:ROWS], both[ROWS:])

    def last_pieces(pieces):
        for p in pieces:
            for direction in both:
                landed(direction, p, 7)
            unpack_both(p, 7)
        for p in pieces:
            landed(p % 2, p, 8)
            unpack_slots(p, [place_at(0, 8)])

    last_pieces((0, 1))

    @pl.loop(0, TILES, unroll=2)
    def _(t):
        first_half[:, pl.ds(pl.multiple_of(t * 128, 128), 128)] = interpolate(t, 0)

    last_pieces((2, 3))

    @pl.loop(0, TILES, unroll=2)
    def _(t):
        lanes = pl.ds(pl.multiple_of(t * 128, 128), 128)
        modelled = first_half[:, lanes] + interpolate(t, 1)
        weight = conf_ref[:, lanes]
        residual = meas_ref[:, lanes] - modelled[24:27]
        sens[:, lanes] = modelled[:24]
        resid[0:3, lanes] = residual
        upper, lower = split_two(modelled[:24])
        norm_l[0:24, lanes] = upper
        norm_l[24:48, lanes] = lower
        weighted = [split_two(modelled[8 * c:8 * c + 8] * weight) for c in range(COMPS)]
        right_side = split_two(residual * weight)
        for part in range(2):
            for c in range(COMPS):
                start = 64 * part + 16 * c
                norm_r[start:start + 8, lanes] = weighted[c][part]
                norm_r[start + 8:start + 9, lanes] = right_side[part][c:c + 1]

    gram = lax.dot_general(
        norm_l[...].astype(BF16), norm_r[...].astype(BF16), (((1,), (1,)), ((), ())), preferred_element_type=F32
    )
    gram = gram[:24] + gram[24:]
    gram = gram + pltpu.roll(gram, 64, 1)
    normal = gram[:8] + pltpu.roll(gram[8:16], 112, 1) + pltpu.roll(gram[16:24], 96, 1)
    sub, lane = iota((8, 128), 0), iota((8, 128), 1)
    normal = jnp.where(lane < 16, normal, 0.0)
    for shift in (16, 32, 64):
        normal = normal + pltpu.roll(normal, shift, 1)
    own_chunk = (lane >> 4) == sub
    red1[me_g] = jnp.sum(jnp.where(own_chunk, normal, 0.0), axis=0, keepdims=True)

    @pl.loop(1, GRP)
    def _(j):
        reduce_copy(red1, r1s, r1r, j, False, True).start()

    def turn(landing, outgoing, comps):
        for c in range(comps):
            for upper_part in range(4):
                for side in range(2):
                    if len(landing.shape) == 2:
                        block = landing[pl.ds(128 * side + 4 * c + upper_part, 8, stride=16), :]
                    else:
                        block = landing[8 * side:8 * side + 8, c, upper_part, :]
                    start = 64 * upper_part + 8 * (4 * side + c)
                    flip[start:start + 8, :] = swap_chunks(block)
        for upper_part in range(4):
            for lower_part in range(8):
                start = 64 * upper_part + 8 * lower_part
                outgoing[start:start + 8, :] = flip[pl.ds(64 * upper_part + lower_part, 8, stride=8), :]

    @pl.loop(1, GRP)
    def _(j):
        reduce_copy(red1, r1s, r1r, j, True, True).wait_recv()

    red2[me_s] = jnp.sum(red1[...], axis=0)

    @pl.loop(1, SLAB)
    def _(j):
        reduce_copy(red2, r2s, r2r, j, False, False).start()

    @pl.loop(1, GRP)
    def _(j):
        group_copy(early_out, early1, e1s, e1r, j, False).start()

    mine = pl.ds(pl.multiple_of(16 * me_g, 16), 16)
    early1[mine, :] = early_out[mine, :]

    @pl.loop(1, SLAB)
    def _(j):
        reduce_copy(red2, r2s, r2r, j, True, False).wait_recv()

    system = jnp.where(own_chunk, jnp.sum(red2[...], axis=0), 0.0)
    for shift in (16, 32, 64):
        system = system + pltpu.roll(system, shift, 1)
    column = lane & 15
    system = jnp.where(column == sub, system * (1.0 + DAMPING), system)
    for i in range(PARAMS):
        factor = system[:, i:i + 1]
        pivot_row = system[i:i + 1, :] / system[i:i + 1, i:i + 1]
        system = jnp.where(sub == i, pivot_row, system - factor * pivot_row)
    update = system[:, 8:9]
    flat = jnp.sum(jnp.where(lane == sub, update, 0.0), axis=0, keepdims=True)
    upd_ref[...] = flat[:, :PARAMS]

    placed = jnp.zeros((6 * HIGH, 128), F32)
    for q in range(8):
        lanes = slice(512 * q, 512 * (q + 1))
        mask = scatter_m[:, lanes]
        pieces = []
        for c in range(COMPS):
            predicted = jnp.sum(sens[8 * c:8 * c + 8, lanes] * update, axis=0, keepdims=True)
            pieces.append(split_two(resid[c:c + 1, lanes] - predicted))
        stacked = jnp.concatenate(
            [mask * pieces[c][part].astype(BF16) for part in range(2) for c in range(COMPS)], axis=0
        )
        placed = placed + jnp.dot(stacked, scatter_b[lanes, :], preferred_element_type=F32)
    placed = placed[:3 * HIGH] + placed[3 * HIGH:]
    for c in range(COMPS):
        for g in range(GRP):
            late_out[g, c] = placed[HIGH * c + 4 * g:HIGH * c + 4 * g + 4, :]

    @pl.loop(1, GRP)
    def _(j):
        group_copy(late_out, late1, d1s, d1r, j, False).start()

    late1[me_g] = late_out[me_g]

    @pl.loop(1, GRP)
    def _(j):
        group_copy(early_out, early1, e1s, e1r, j, True).wait_recv()

    turn(early1, early2_out, 4)

    @pl.loop(1, SLAB)
    def _(j):
        slab_copy(early2_out, early2, e2s, e2r, j, False).start()

    own_rows = pl.ds(pl.multiple_of(8 * me_s, 8), 8)
    early2[own_rows, :] = early2_out[own_rows, :]

    @pl.loop(1, GRP)
    def _(j):
        group_copy(late_out, late1, d1s, d1r, j, True).wait_recv()

    turn(late1, late2_out, 3)

    @pl.loop(1, SLAB)
    def _(j):
        slab_copy(late2_out, late2, d2s, d2r, j, False).start()

    late2[own_rows, :] = late2_out[own_rows, :]

    @pl.loop(1, SLAB)
    def _(j):
        slab_copy(early2_out, early2, e2s, e2r, j, True).wait_recv()

    @pl.loop(1, SLAB)
    def _(j):
        slab_copy(late2_out, late2, d2s, d2r, j, True).wait_recv()

    for first in range(0, SLAB, 8):
        for side in range(2):
            def rows_of(ref, c):
                return ref[pl.ds(8 * first + 4 * side + c, 8, stride=8), :]

            confidence = rows_of(early2, 3)
            squares = jnp.zeros_like(confidence)
            results = []
            late_rows = [rows_of(late2, c) for c in range(COMPS)]
            for c in range(COMPS):
                results.append(rows_of(early2, c) - late_rows[c])
            for c in range(COMPS):
                results.append(confidence * late_rows[c])
                squares = squares + late_rows[c] * late_rows[c]
            results.append(confidence)
            results.append(confidence * squares)
            for r in range(8):
                flip[8 * r:8 * r + 8, :] = results[r]
            for n in range(8):
                start = 256 * (first + n) + 128 * side
                out_ref[:, start:start + 128] = flip[pl.ds(n, 8, stride=8), :]

    for p in range(PIECES):
        for direction in both:
            @pl.loop(1, 9 if p % 2 == direction else 8)
            def _(position):
                hop(direction, p, position - 1, 1).wait_send()

    @pl.loop(1, GRP)
    def _(j):
        group_copy(early_out, early1, e1s, e1r, j, False).wait_send()
        group_copy(late_out, late1, d1s, d1r, j, False).wait_send()
        reduce_copy(red1, r1s, r1r, j, False, True).wait_send()

    @pl.loop(1, SLAB)
    def _(j):
        slab_copy(early2_out, early2, e2s, e2r, j, False).wait_send()
        slab_copy(late2_out, late2, d2s, d2r, j, False).wait_send()
        reduce_copy(red2, r2s, r2r, j, False, False).wait_send()


def body(fields, spline, measured, confidence, block_ids, live, owners):
    vmem = pl.BlockSpec(memory_space=pltpu.VMEM)
    smem = pl.BlockSpec(memory_space=pltpu.SMEM)
    dma = pltpu.SemaphoreType.DMA
    received, update = pl.pallas_call(
        kernel,
        out_shape=(
            jax.ShapeDtypeStruct((8, PEERS * CAP), F32),
            jax.ShapeDtypeStruct((1, PARAMS), F32),
        ),
        in_specs=[smem, smem, vmem, pl.BlockSpec(memory_space=pl.ANY), vmem, vmem, vmem],
        out_specs=(vmem, vmem),
        scratch_shapes=[
            pltpu.VMEM((3, 8, SLOTS, SUBSETS), BF16),
            dma,
            pltpu.VMEM((PIECES, GRP, PACKED, PIECE), BF16),
            pltpu.VMEM((PIECES, GRP * BLOCKS, ROWS, PIECE), BF16),
            pltpu.VMEM((TILES, SLOTS * BLK, 128), BF16),
            pltpu.VMEM((3, 32, 128), F32),
            pltpu.VMEM((PEERS, 128), F32),
            pltpu.VMEM((CHUNK, CHUNK + 128), BF16),
            pltpu.VMEM((BLOCKS * ROWS, PACKED), BF16),
            pltpu.VMEM((SUBSETS, 128), BF16),
            pltpu.VMEM((HIGH, SUBSETS), BF16),
            pltpu.VMEM((8 * HIGH, 128), F32),
            pltpu.VMEM((ROWS, SUBSETS), F32),
            pltpu.VMEM((24, SUBSETS), F32),
            pltpu.VMEM((8, SUBSETS), F32),
            pltpu.VMEM((48, SUBSETS), F32),
            pltpu.VMEM((128, SUBSETS), F32),
            pltpu.VMEM((GRP, 1, 128), F32),
            pltpu.VMEM((SLAB, 1, 128), F32),
            pltpu.VMEM((GRP * 16, 128), F32),
            pltpu.VMEM((GRP * 16, 128), F32),
            pltpu.VMEM((SLAB * 8, 128), F32),
            pltpu.VMEM((SLAB * 8, 128), F32),
            pltpu.VMEM((GRP, COMPS, 4, 128), F32),
            pltpu.VMEM((GRP, COMPS, 4, 128), F32),
            pltpu.VMEM((SLAB * 8, 128), F32),
            pltpu.VMEM((SLAB * 8, 128), F32),
            pltpu.VMEM((256, 128), F32),
            dma((2, PIECES, 9)), dma((2, PIECES, 9)),
            dma((GRP,)), dma((GRP,)), dma((SLAB,)), dma((SLAB,)),
            dma((GRP,)), dma((GRP,)), dma((SLAB,)), dma((SLAB,)),
            dma((GRP,)), dma((GRP,)), dma((SLAB,)), dma((SLAB,)),
        ],
        compiler_params=pltpu.CompilerParams(
            collective_id=0, has_side_effects=True, vmem_limit_bytes=56 * 1024 * 1024
        ),
    )(
        block_ids.T, live, fields, spline, measured,
        confidence.reshape(1, SUBSETS), owners.reshape(1, SUBSETS),
    )
    return (received, update.reshape(PARAMS))


def solution(mesh):
    placed = (
        P(None, ("slab", "grp")),
        P(None, None, None, ("slab", "grp")),
        P(None, ("slab", "grp")),
        P(("slab", "grp")),
        P(("slab", "grp"), None),
        P(("slab", "grp")),
        P(("slab", "grp"), None),
    )
    return jax.shard_map(
        body, mesh=mesh, in_specs=placed, out_specs=(P(None, ("slab", "grp")), P()), check_vma=False
    )
```

```python
import functools

import jax
import jax.numpy as jnp
from jax import lax
from jax.experimental import pallas as pl
from jax.experimental.pallas import tpu as pltpu
from jax.sharding import PartitionSpec as P

MESH = pl.DeviceIdType.MESH
F32 = jnp.float32
BF16 = jnp.bfloat16
DAMPING = 0.05

PARAMS = 8
COMPS = 3
CHANNELS = 27
ROWS = 32
BLOCKS = 4
PACKED = 112
BLK = 512
PIECE = 128
PIECES = 4
STEPS = 6
SLOTS = 4
CAP = 16
GRP = 16
SLAB = 32
SUBSETS = 4096
CHUNK = 256
CHUNKS = 16
PEERS = 512
HIGH = 64


def iota(shape, axis):
    return lax.broadcasted_iota(jnp.int32, shape, axis)


def split_two(value):
    upper = value.astype(BF16).astype(F32)
    return upper, (value - upper).astype(BF16).astype(F32)


def swap_chunks(value):
    sub, lane = iota((8, 128), 0), iota((8, 128), 1)
    for bit in range(3):
        step = 1 << bit
        sub_bit, lane_bit = (sub >> bit) & 1, (lane >> (4 + bit)) & 1
        upward = pltpu.roll(pltpu.roll(value, 16 * step, 1), 8 - step, 0)
        downward = pltpu.roll(pltpu.roll(value, 128 - 16 * step, 1), step, 0)
        value = jnp.where(sub_bit == lane_bit, value, jnp.where(sub_bit == 0, upward, downward))
    return value


def kernel(
    ids_ref, live_ref, fields_ref, spline_hbm, meas_ref, conf_ref, own_ref,
    out_ref, upd_ref,
    spline_ref, spline_sem, land, store, tiles, sp32, carry, upper_ref, unpack_ref,
    scatter_b, scatter_m, early_acc, first_half, sens, resid, gram_ref,
    red1, red2, early_out, early1, early2_out, early2, late_out, late1, late2_out, late2, flip,
    ag_send, ag_recv, r1s, r1r, r2s, r2r, e1s, e1r, e2s, e2r, d1s, d1r, d2s, d2r,
):
    me_s = lax.axis_index("slab")
    me_g = lax.axis_index("grp")

    barrier = pltpu.get_barrier_semaphore()

    for j in (1, 2, GRP - 2, GRP - 1):
        pl.semaphore_signal(barrier, inc=1, device_id=(me_s, lax.rem(me_g + j, GRP)), device_id_type=MESH)

    @pl.loop(1, SLAB)
    def _(j):
        pl.semaphore_signal(barrier, inc=1, device_id=(lax.rem(me_s + j, SLAB), me_g), device_id_type=MESH)

    spline_copy = pltpu.make_async_copy(spline_hbm, spline_ref, spline_sem)
    spline_copy.start()

    row = iota((PACKED, CHANNELS), 0)
    channel = iota((PACKED, CHANNELS), 1)
    packed = None
    for j in range(BLOCKS):
        new = row - CHANNELS * j
        source = jnp.where(new < 24, 3 + 3 * (new & 7) + (new >> 3), new - 24)
        pick = (channel == source) & (new >= 0) & (new < CHANNELS)
        part = jnp.dot(
            jnp.where(pick, 1.0, 0.0).astype(BF16), fields_ref[:, j * BLK:(j + 1) * BLK], preferred_element_type=F32
        )
        packed = part if packed is None else packed + part
    packed = packed.astype(BF16)
    for p in range(PIECES):
        land[p, me_g] = packed[:, p * PIECE:(p + 1) * PIECE]

    def place_at(direction, distance):
        return lax.rem(me_g + (distance if direction == 0 else GRP - distance), GRP)

    def hop(direction, p, position, reach):
        slot = place_at(1 - direction, position)
        return pltpu.make_async_remote_copy(
            src_ref=land.at[p, slot], dst_ref=land.at[p, slot],
            send_sem=ag_send.at[direction, p, position + reach], recv_sem=ag_recv.at[direction, p, position + reach],
            device_id=(me_s, place_at(direction, reach)), device_id_type=MESH,
        )

    def landed(direction, p, position):
        slot = place_at(1 - direction, position)
        pltpu.make_async_remote_copy(
            src_ref=land.at[p, slot], dst_ref=land.at[p, slot],
            send_sem=ag_send.at[direction, p, position], recv_sem=ag_recv.at[direction, p, position],
            device_id=(me_s, place_at(direction, 1)), device_id_type=MESH,
        ).wait_recv()

    def unpack_slots(p, slots):
        joined = jnp.concatenate([land[p, slot] for slot in slots], axis=1)
        rows = jnp.dot(unpack_ref[...], joined, preferred_element_type=F32).astype(BF16)
        for n, slot in enumerate(slots):
            part = rows[:, n * PIECE:(n + 1) * PIECE].reshape(BLOCKS, ROWS, PIECE)
            store[p, pl.ds(BLOCKS * slot, BLOCKS)] = part

    def build_tile(j, side):
        t = 2 * j + side
        lanes = pl.ds(pl.multiple_of(t * 128, 128), 128)
        for axis in range(3):
            part = spline_ref[axis, :, :, lanes].astype(F32)
            for e in range(8):
                sp32[axis, e * 4:(e + 1) * 4, :] = part[e]
        live_row = jnp.where(iota((8, 128), 1) < 64, live_ref[2 * t], live_ref[2 * t + 1])
        for k in range(SLOTS):
            along_z = sp32[0, pl.ds(k, 8, stride=4), :]
            along_y = sp32[1, pl.ds(k, 8, stride=4), :]
            along_x = sp32[2, pl.ds(k, 8, stride=4), :]
            along_z = jnp.where(live_row > k, along_z, 0.0)
            for z in range(8):
                face = along_z[z:z + 1, :] * along_y
                cells = (face[:, None, :] * along_x[None, :, :]).reshape(64, 128)
                start = (z // 2) * 512 + k * PIECE + (z % 2) * 64
                tiles[j, start:start + 64, 128 * side:128 * side + 128] = cells.astype(BF16)

    def place_chunk(j):
        lanes = pl.ds(pl.multiple_of(j * CHUNK, CHUNK), CHUNK)
        owner = own_ref[:, lanes]
        onehot = jnp.where(iota((PEERS, CHUNK), 0) == owner, 1.0, 0.0)
        counted = jnp.dot(onehot.astype(BF16), upper_ref[...], preferred_element_type=F32)
        before = carry[...]
        rank = jnp.sum(
            onehot * (counted[:, :CHUNK] + jnp.concatenate([before, before], axis=1)), axis=0, keepdims=True
        )
        carry[...] = before + counted[:, CHUNK:]
        low = ((owner >> 4) & 7) * CAP + rank.astype(jnp.int32)
        high = (owner & 15) * 4 + (owner >> 7)
        column = jnp.where(iota((128, CHUNK), 0) == low, 1.0, 0.0).T.astype(BF16)
        scatter_b[lanes, :] = column
        mask = jnp.where(iota((HIGH, CHUNK), 0) == high, 1.0, 0.0).astype(BF16)
        scatter_m[:, lanes] = mask
        pieces = []
        for value in [meas_ref[c:c + 1, lanes] for c in range(COMPS)] + [conf_ref[:, lanes]]:
            pieces.append(split_two(value))
        stacked = jnp.concatenate(
            [mask * pieces[c][part].astype(BF16) for part in range(2) for c in range(4)], axis=0
        )
        early_acc[...] += jnp.dot(stacked, column, preferred_element_type=F32)

    pl.semaphore_wait(barrier, SLAB + 3)

    both = (0, 1)

    def send_step(p, step, position):
        for direction in both:
            @pl.when((step < STEPS - 1) | (p % 2 == direction))
            def _():
                hop(direction, p, position, 1 + (step % 3) // 2).start()

            @pl.when(step % 3 == 2)
            def _():
                hop(direction, p, position, 1).start()

    for p in range(PIECES):
        for direction in both:
            hop(direction, p, 0, 1).start()

    row, col = iota((CHUNK, CHUNK + 128), 0), iota((CHUNK, CHUNK + 128), 1)
    upper_ref[...] = jnp.where((row < col) | (col >= CHUNK), 1.0, 0.0).astype(BF16)
    row, col = iota((BLOCKS * ROWS, PACKED), 0), iota((BLOCKS * ROWS, PACKED), 1)
    unpack = jnp.zeros((BLOCKS * ROWS, PACKED), F32)
    for j in range(BLOCKS):
        inside = (row >= ROWS * j) & (row < ROWS * j + CHANNELS)
        unpack = jnp.where(inside & (col == row - (ROWS - CHANNELS) * j), 1.0, unpack)
    unpack_ref[...] = unpack.astype(BF16)
    carry[...] = jnp.zeros_like(carry)
    early_acc[...] = jnp.zeros_like(early_acc)

    def build(lo, hi):
        @pl.loop(lo, hi)
        def _(j):
            build_tile(j, 0)
            build_tile(j, 1)
            place_chunk(j)

    def unpack_both(p, position):
        unpack_slots(p, [place_at(0, position), place_at(1, position)])

    spline_copy.wait()
    for p in range(PIECES):
        unpack_slots(p, [me_g])
    build(0, 2)

    @pl.loop(1, STEPS)
    def _(step):
        position = step + step // 3
        for group in range(2):
            pieces = (2 * group, 2 * group + 1)
            for p in pieces:
                for direction in both:
                    landed(direction, p, position)
                send_step(p, step, position)
            for p in pieces:
                unpack_both(p, position)

            @pl.when(step == 3)
            def _():
                for p in pieces:
                    for direction in both:
                        landed(direction, p, 3)
                    unpack_both(p, 3)

            turn_index = 2 * (step - 1) + group
            build(2 + (turn_index * 7) // 5, 2 + ((turn_index + 1) * 7) // 5)

    total = early_acc[0:4 * HIGH, :] + early_acc[4 * HIGH:, :]
    for c in range(4):
        for g in range(GRP):
            early_out[16 * g + 4 * c:16 * g + 4 * c + 4, :] = total[HIGH * c + 4 * g:HIGH * c + 4 * g + 4, :]

    def far_group(n):
        return GRP // 2 + (n // 2) * (2 * (n % 2) - 1)

    def far_slab(n):
        def order(k):
            return (18 - k - k * (k - 1) // 2) % 4

        x, y = (me_s // 8 + order(n // 8)) % 4, ((me_s // 2) % 4 + order((n // 2) % 4)) % 4
        return x * 8 + y * 2 + (me_s + 1 + n) % 2

    def group_copy(source, landing, send, recv, j, arriving):
        peer = lax.rem(me_g + j, GRP)
        origin = peer if arriving else me_g
        flat = len(source.shape) == 2
        return pltpu.make_async_remote_copy(
            src_ref=source.at[pl.ds(pl.multiple_of(16 * peer, 16), 16)] if flat else source.at[peer],
            dst_ref=landing.at[pl.ds(pl.multiple_of(16 * origin, 16), 16)] if flat else landing.at[origin],
            send_sem=send.at[peer], recv_sem=recv.at[origin],
            device_id=(me_s, peer), device_id_type=MESH,
        )

    def slab_copy(source, landing, send, recv, j, arriving):
        peer = lax.rem(me_s + j, SLAB)
        origin = peer if arriving else me_s
        return pltpu.make_async_remote_copy(
            src_ref=source.at[pl.ds(pl.multiple_of(8 * peer, 8), 8)],
            dst_ref=landing.at[pl.ds(pl.multiple_of(8 * origin, 8), 8)],
            send_sem=send.at[peer], recv_sem=recv.at[origin],
            device_id=(peer, me_g), device_id_type=MESH,
        )

    def reduce_copy(buffer, send, recv, j, arriving, along_group):
        size = GRP if along_group else SLAB
        mine = me_g if along_group else me_s
        peer = lax.rem(mine + j, size)
        origin = peer if arriving else mine
        return pltpu.make_async_remote_copy(
            src_ref=buffer.at[origin], dst_ref=buffer.at[origin],
            send_sem=send.at[peer], recv_sem=recv.at[origin],
            device_id=(me_s, peer) if along_group else (peer, me_g), device_id_type=MESH,
        )

    def interpolate(j, half):
        rows = []
        for n in range(4):
            rows.append(
                jnp.concatenate(
                    [store[p, ids_ref[k, 4 * j + n]] for p in (2 * half, 2 * half + 1) for k in range(SLOTS)], axis=1
                )
            )
        crossed = jnp.dot(
            jnp.concatenate(rows, axis=0), tiles[j, 1024 * half:1024 * half + 1024], preferred_element_type=F32
        )
        left_block = iota((ROWS, 128), 1) < 64
        sides = []
        for side in range(2):
            part = crossed[2 * ROWS * side:2 * ROWS * side + 2 * ROWS, 128 * side:128 * side + 128]
            sides.append(jnp.where(left_block, part[:ROWS], part[ROWS:]))
        return jnp.concatenate(sides, axis=1)

    def last_pieces(pieces):
        for p in pieces:
            for direction in both:
                landed(direction, p, 7)
            unpack_both(p, 7)
        for p in pieces:
            landed(p % 2, p, 8)
            unpack_slots(p, [place_at(0, 8)])

    last_pieces((0, 1))

    @pl.loop(0, CHUNKS, unroll=2)
    def _(j):
        first_half[:, pl.ds(pl.multiple_of(j * CHUNK, CHUNK), CHUNK)] = interpolate(j, 0)

    last_pieces((2, 3))

    gram_ref[...] = jnp.zeros_like(gram_ref)

    @pl.loop(0, CHUNKS, unroll=2)
    def _(j):
        lanes = pl.ds(pl.multiple_of(j * CHUNK, CHUNK), CHUNK)
        modelled = first_half[:, lanes] + interpolate(j, 1)
        weight = conf_ref[:, lanes]
        residual = meas_ref[:, lanes] - modelled[24:27]
        sens[:, lanes] = modelled[:24]
        resid[0:3, lanes] = residual
        left_side = jnp.concatenate(split_two(modelled[:24]), axis=0).astype(BF16)
        zeros = jnp.zeros((7, CHUNK), F32)
        weighted = jnp.concatenate(
            [
                piece
                for c in range(COMPS)
                for piece in (modelled[8 * c:8 * c + 8] * weight, residual[c:c + 1] * weight, zeros)
            ] + [jnp.zeros((16, CHUNK), F32)],
            axis=0,
        )
        right_side = jnp.concatenate(split_two(weighted), axis=0).astype(BF16)
        gram_ref[...] += lax.dot_general(
            left_side, right_side, (((1,), (1,)), ((), ())), preferred_element_type=F32
        )

    gram = gram_ref[...]
    gram = gram[:24] + gram[24:]
    gram = gram + pltpu.roll(gram, 64, 1)
    normal = gram[:8] + pltpu.roll(gram[8:16], 112, 1) + pltpu.roll(gram[16:24], 96, 1)
    sub, lane = iota((8, 128), 0), iota((8, 128), 1)
    normal = jnp.where(lane < 16, normal, 0.0)
    for shift in (16, 32, 64):
        normal = normal + pltpu.roll(normal, shift, 1)
    own_chunk = (lane >> 4) == sub
    red1[me_g] = jnp.sum(jnp.where(own_chunk, normal, 0.0), axis=0, keepdims=True)

    @pl.loop(1, GRP)
    def _(j):
        reduce_copy(red1, r1s, r1r, far_group(j), False, True).start()

    def turn(landing, outgoing, comps):
        for c in range(comps):
            for upper_part in range(4):
                for side in range(2):
                    if len(landing.shape) == 2:
                        block = landing[pl.ds(128 * side + 4 * c + upper_part, 8, stride=16), :]
                    else:
                        block = landing[8 * side:8 * side + 8, c, upper_part, :]
                    start = 64 * upper_part + 8 * (4 * side + c)
                    flip[start:start + 8, :] = swap_chunks(block)
        for upper_part in range(4):
            for lower_part in range(8):
                start = 64 * upper_part + 8 * lower_part
                outgoing[start:start + 8, :] = flip[pl.ds(64 * upper_part + lower_part, 8, stride=8), :]

    @pl.loop(1, GRP)
    def _(j):
        reduce_copy(red1, r1s, r1r, j, True, True).wait_recv()

    red2[me_s] = jnp.sum(red1[...], axis=0)

    @pl.loop(0, SLAB - 1)
    def _(j):
        reduce_copy(red2, r2s, r2r, far_slab(j) + SLAB - me_s, False, False).start()

    @pl.loop(1, GRP)
    def _(j):
        group_copy(early_out, early1, e1s, e1r, far_group(j), False).start()

    mine = pl.ds(pl.multiple_of(16 * me_g, 16), 16)
    early1[mine, :] = early_out[mine, :]

    @pl.loop(1, SLAB)
    def _(j):
        reduce_copy(red2, r2s, r2r, j, True, False).wait_recv()

    system = jnp.where(own_chunk, jnp.sum(red2[...], axis=0), 0.0)
    for shift in (16, 32, 64):
        system = system + pltpu.roll(system, shift, 1)
    column = lane & 15
    system = jnp.where(column == sub, system * (1.0 + DAMPING), system)
    for i in range(PARAMS):
        factor = system[:, i:i + 1]
        pivot_row = system[i:i + 1, :] / system[i:i + 1, i:i + 1]
        system = jnp.where(sub == i, pivot_row, system - factor * pivot_row)
    update = system[:, 8:9]
    flat = jnp.sum(jnp.where(lane == sub, update, 0.0), axis=0, keepdims=True)
    upd_ref[...] = flat[:, :PARAMS]

    placed = jnp.zeros((6 * HIGH, 128), F32)
    for q in range(8):
        lanes = slice(512 * q, 512 * (q + 1))
        mask = scatter_m[:, lanes]
        pieces = []
        for c in range(COMPS):
            predicted = jnp.sum(sens[8 * c:8 * c + 8, lanes] * update, axis=0, keepdims=True)
            pieces.append(split_two(resid[c:c + 1, lanes] - predicted))
        stacked = jnp.concatenate(
            [mask * pieces[c][part].astype(BF16) for part in range(2) for c in range(COMPS)], axis=0
        )
        placed = placed + jnp.dot(stacked, scatter_b[lanes, :], preferred_element_type=F32)
    placed = placed[:3 * HIGH] + placed[3 * HIGH:]
    for c in range(COMPS):
        for g in range(GRP):
            late_out[g, c] = placed[HIGH * c + 4 * g:HIGH * c + 4 * g + 4, :]

    @pl.loop(1, GRP)
    def _(j):
        group_copy(late_out, late1, d1s, d1r, far_group(j), False).start()

    late1[me_g] = late_out[me_g]

    @pl.loop(1, GRP)
    def _(j):
        group_copy(early_out, early1, e1s, e1r, j, True).wait_recv()

    turn(early1, early2_out, 4)

    @pl.loop(0, SLAB - 1)
    def _(j):
        slab_copy(early2_out, early2, e2s, e2r, far_slab(j) + SLAB - me_s, False).start()

    own_rows = pl.ds(pl.multiple_of(8 * me_s, 8), 8)
    early2[own_rows, :] = early2_out[own_rows, :]

    @pl.loop(1, GRP)
    def _(j):
        group_copy(late_out, late1, d1s, d1r, j, True).wait_recv()

    turn(late1, late2_out, 3)

    @pl.loop(0, SLAB - 1)
    def _(j):
        slab_copy(late2_out, late2, d2s, d2r, far_slab(j) + SLAB - me_s, False).start()

    late2[own_rows, :] = late2_out[own_rows, :]

    @pl.loop(1, SLAB)
    def _(j):
        slab_copy(early2_out, early2, e2s, e2r, j, True).wait_recv()

    @pl.loop(1, SLAB)
    def _(j):
        slab_copy(late2_out, late2, d2s, d2r, j, True).wait_recv()

    for first in range(0, SLAB, 8):
        for side in range(2):
            def rows_of(ref, c):
                return ref[pl.ds(8 * first + 4 * side + c, 8, stride=8), :]

            confidence = rows_of(early2, 3)
            squares = jnp.zeros_like(confidence)
            results = []
            late_rows = [rows_of(late2, c) for c in range(COMPS)]
            for c in range(COMPS):
                results.append(rows_of(early2, c) - late_rows[c])
            for c in range(COMPS):
                results.append(confidence * late_rows[c])
                squares = squares + late_rows[c] * late_rows[c]
            results.append(confidence)
            results.append(confidence * squares)
            for r in range(8):
                flip[8 * r:8 * r + 8, :] = results[r]
            for n in range(8):
                start = 256 * (first + n) + 128 * side
                out_ref[:, start:start + 128] = flip[pl.ds(n, 8, stride=8), :]

    for p in range(PIECES):
        for direction in both:
            @pl.loop(1, 9 if p % 2 == direction else 8)
            def _(position):
                hop(direction, p, position - 1, 1).wait_send()

    @pl.loop(1, GRP)
    def _(j):
        group_copy(early_out, early1, e1s, e1r, j, False).wait_send()
        group_copy(late_out, late1, d1s, d1r, j, False).wait_send()
        reduce_copy(red1, r1s, r1r, j, False, True).wait_send()

    @pl.loop(1, SLAB)
    def _(j):
        slab_copy(early2_out, early2, e2s, e2r, j, False).wait_send()
        slab_copy(late2_out, late2, d2s, d2r, j, False).wait_send()
        reduce_copy(red2, r2s, r2r, j, False, False).wait_send()


def body(fields, spline, measured, confidence, block_ids, live, owners):
    vmem = pl.BlockSpec(memory_space=pltpu.VMEM)
    smem = pl.BlockSpec(memory_space=pltpu.SMEM)
    dma = pltpu.SemaphoreType.DMA
    received, update = pl.pallas_call(
        kernel,
        out_shape=(
            jax.ShapeDtypeStruct((8, PEERS * CAP), F32),
            jax.ShapeDtypeStruct((1, PARAMS), F32),
        ),
        in_specs=[smem, smem, vmem, pl.BlockSpec(memory_space=pl.ANY), vmem, vmem, vmem],
        out_specs=(vmem, vmem),
        scratch_shapes=[
            pltpu.VMEM((3, 8, SLOTS, SUBSETS), BF16),
            dma,
            pltpu.VMEM((PIECES, GRP, PACKED, PIECE), BF16),
            pltpu.VMEM((PIECES, GRP * BLOCKS, ROWS, PIECE), BF16),
            pltpu.VMEM((CHUNKS, SLOTS * BLK, CHUNK), BF16),
            pltpu.VMEM((3, 32, 128), F32),
            pltpu.VMEM((PEERS, 128), F32),
            pltpu.VMEM((CHUNK, CHUNK + 128), BF16),
            pltpu.VMEM((BLOCKS * ROWS, PACKED), BF16),
            pltpu.VMEM((SUBSETS, 128), BF16),
            pltpu.VMEM((HIGH, SUBSETS), BF16),
            pltpu.VMEM((8 * HIGH, 128), F32),
            pltpu.VMEM((ROWS, SUBSETS), F32),
            pltpu.VMEM((24, SUBSETS), F32),
            pltpu.VMEM((8, SUBSETS), F32),
            pltpu.VMEM((48, 128), F32),
            pltpu.VMEM((GRP, 1, 128), F32),
            pltpu.VMEM((SLAB, 1, 128), F32),
            pltpu.VMEM((GRP * 16, 128), F32),
            pltpu.VMEM((GRP * 16, 128), F32),
            pltpu.VMEM((SLAB * 8, 128), F32),
            pltpu.VMEM((SLAB * 8, 128), F32),
            pltpu.VMEM((GRP, COMPS, 4, 128), F32),
            pltpu.VMEM((GRP, COMPS, 4, 128), F32),
            pltpu.VMEM((SLAB * 8, 128), F32),
            pltpu.VMEM((SLAB * 8, 128), F32),
            pltpu.VMEM((256, 128), F32),
            dma((2, PIECES, 9)), dma((2, PIECES, 9)),
            dma((GRP,)), dma((GRP,)), dma((SLAB,)), dma((SLAB,)),
            dma((GRP,)), dma((GRP,)), dma((SLAB,)), dma((SLAB,)),
            dma((GRP,)), dma((GRP,)), dma((SLAB,)), dma((SLAB,)),
        ],
        compiler_params=pltpu.CompilerParams(
            collective_id=0, has_side_effects=True, vmem_limit_bytes=56 * 1024 * 1024
        ),
    )(
        block_ids.T, live, fields, spline, measured,
        confidence.reshape(1, SUBSETS), owners.reshape(1, SUBSETS),
    )
    return (received, update.reshape(PARAMS))


def solution(mesh):
    placed = (
        P(None, ("slab", "grp")),
        P(None, None, None, ("slab", "grp")),
        P(None, ("slab", "grp")),
        P(("slab", "grp")),
        P(("slab", "grp"), None),
        P(("slab", "grp")),
        P(("slab", "grp"), None),
    )
    return jax.shard_map(
        body, mesh=mesh, in_specs=placed, out_specs=(P(None, ("slab", "grp")), P()), check_vma=False
    )
```

```python
import functools

import jax
import jax.numpy as jnp
from jax import lax
from jax.experimental import pallas as pl
from jax.experimental.pallas import tpu as pltpu
from jax.sharding import PartitionSpec as P

MESH = pl.DeviceIdType.MESH
F32 = jnp.float32
BF16 = jnp.bfloat16
DAMPING = 0.05

PARAMS = 8
COMPS = 3
CHANNELS = 27
ROWS = 32
BLOCKS = 4
PACKED = 112
BLK = 512
PIECE = 128
PIECES = 4
STEPS = 6
SLOTS = 4
CAP = 16
GRP = 16
SLAB = 32
SUBSETS = 4096
CHUNK = 256
CHUNKS = 16
PEERS = 512
HIGH = 32
LOW = 256


def iota(shape, axis):
    return lax.broadcasted_iota(jnp.int32, shape, axis)


def split_two(value):
    upper = value.astype(BF16).astype(F32)
    return upper, (value - upper).astype(BF16).astype(F32)


def swap_chunks(value):
    sub, lane = iota((8, 128), 0), iota((8, 128), 1)
    for bit in range(3):
        step = 1 << bit
        sub_bit, lane_bit = (sub >> bit) & 1, (lane >> (4 + bit)) & 1
        upward = pltpu.roll(pltpu.roll(value, 16 * step, 1), 8 - step, 0)
        downward = pltpu.roll(pltpu.roll(value, 128 - 16 * step, 1), step, 0)
        value = jnp.where(sub_bit == lane_bit, value, jnp.where(sub_bit == 0, upward, downward))
    return value


def kernel(
    ids_ref, live_ref, fields_ref, spline_hbm, meas_ref, conf_ref, own_ref,
    out_ref, upd_ref,
    spline_ref, spline_sem, land, store, tiles, sp32, carry, upper_ref, unpack_ref,
    scatter_b, scatter_m, early_acc, first_half, sens, resid, gram_ref,
    red1, red2, early_out, early1, early2_out, early2, late_out, late1, late2_out, late2, flip,
    ag_send, ag_recv, r1s, r1r, r2s, r2r, e1s, e1r, e2s, e2r, d1s, d1r, d2s, d2r,
):
    me_s = lax.axis_index("slab")
    me_g = lax.axis_index("grp")

    barrier = pltpu.get_barrier_semaphore()

    for j in (1, 2, GRP - 2, GRP - 1):
        pl.semaphore_signal(barrier, inc=1, device_id=(me_s, lax.rem(me_g + j, GRP)), device_id_type=MESH)

    @pl.loop(1, SLAB)
    def _(j):
        pl.semaphore_signal(barrier, inc=1, device_id=(lax.rem(me_s + j, SLAB), me_g), device_id_type=MESH)

    spline_copy = pltpu.make_async_copy(spline_hbm, spline_ref, spline_sem)
    spline_copy.start()

    row = iota((PACKED, CHANNELS), 0)
    channel = iota((PACKED, CHANNELS), 1)
    packed = None
    for j in range(BLOCKS):
        new = row - CHANNELS * j
        source = jnp.where(new < 24, 3 + 3 * (new & 7) + (new >> 3), new - 24)
        pick = (channel == source) & (new >= 0) & (new < CHANNELS)
        part = jnp.dot(
            jnp.where(pick, 1.0, 0.0).astype(BF16), fields_ref[:, j * BLK:(j + 1) * BLK], preferred_element_type=F32
        )
        packed = part if packed is None else packed + part
    packed = packed.astype(BF16)
    for p in range(PIECES):
        land[p, me_g] = packed[:, p * PIECE:(p + 1) * PIECE]

    def place_at(direction, distance):
        return lax.rem(me_g + (distance if direction == 0 else GRP - distance), GRP)

    def hop(direction, p, position, reach):
        slot = place_at(1 - direction, position)
        return pltpu.make_async_remote_copy(
            src_ref=land.at[p, slot], dst_ref=land.at[p, slot],
            send_sem=ag_send.at[direction, p, position + reach], recv_sem=ag_recv.at[direction, p, position + reach],
            device_id=(me_s, place_at(direction, reach)), device_id_type=MESH,
        )

    def landed(direction, p, position):
        slot = place_at(1 - direction, position)
        pltpu.make_async_remote_copy(
            src_ref=land.at[p, slot], dst_ref=land.at[p, slot],
            send_sem=ag_send.at[direction, p, position], recv_sem=ag_recv.at[direction, p, position],
            device_id=(me_s, place_at(direction, 1)), device_id_type=MESH,
        ).wait_recv()

    def unpack_slots(p, slots):
        joined = jnp.concatenate([land[p, slot] for slot in slots], axis=1)
        rows = jnp.dot(unpack_ref[...], joined, preferred_element_type=F32).astype(BF16)
        for n, slot in enumerate(slots):
            part = rows[:, n * PIECE:(n + 1) * PIECE].reshape(BLOCKS, ROWS, PIECE)
            store[p, pl.ds(BLOCKS * slot, BLOCKS)] = part

    def build_tile(j, side):
        t = 2 * j + side
        lanes = pl.ds(pl.multiple_of(t * 128, 128), 128)
        for axis in range(3):
            part = spline_ref[axis, :, :, lanes].astype(F32)
            for e in range(8):
                sp32[axis, e * 4:(e + 1) * 4, :] = part[e]
        live_row = jnp.where(iota((8, 128), 1) < 64, live_ref[2 * t], live_ref[2 * t + 1])
        for k in range(SLOTS):
            along_z = sp32[0, pl.ds(k, 8, stride=4), :]
            along_y = sp32[1, pl.ds(k, 8, stride=4), :]
            along_x = sp32[2, pl.ds(k, 8, stride=4), :]
            along_z = jnp.where(live_row > k, along_z, 0.0)
            for z in range(8):
                face = along_z[z:z + 1, :] * along_y
                cells = (face[:, None, :] * along_x[None, :, :]).reshape(64, 128)
                start = (z // 2) * 512 + k * PIECE + (z % 2) * 64
                tiles[j, start:start + 64, 128 * side:128 * side + 128] = cells.astype(BF16)

    def place_chunk(j):
        lanes = pl.ds(pl.multiple_of(j * CHUNK, CHUNK), CHUNK)
        owner = own_ref[:, lanes]
        onehot = jnp.where(iota((PEERS, CHUNK), 0) == owner, 1.0, 0.0)
        counted = jnp.dot(onehot.astype(BF16), upper_ref[...], preferred_element_type=F32)
        before = carry[...]
        rank = jnp.sum(
            onehot * (counted[:, :CHUNK] + jnp.concatenate([before, before], axis=1)), axis=0, keepdims=True
        )
        carry[...] = before + counted[:, CHUNK:]
        low = (owner >> 8) * 128 + ((owner >> 4) & 7) * CAP + rank.astype(jnp.int32)
        high = (owner & 15) * 2 + ((owner >> 7) & 1)
        column = jnp.where(iota((LOW, CHUNK), 0) == low, 1.0, 0.0).T.astype(BF16)
        scatter_b[lanes, :] = column
        mask = jnp.where(iota((HIGH, CHUNK), 0) == high, 1.0, 0.0).astype(BF16)
        scatter_m[:, lanes] = mask
        pieces = []
        for value in [meas_ref[c:c + 1, lanes] for c in range(COMPS)] + [conf_ref[:, lanes]]:
            pieces.append(split_two(value))
        stacked = jnp.concatenate(
            [mask * pieces[c][part].astype(BF16) for part in range(2) for c in range(4)], axis=0
        )
        early_acc[...] += jnp.dot(stacked, column, preferred_element_type=F32)

    pl.semaphore_wait(barrier, SLAB + 3)

    both = (0, 1)

    def send_step(direction, p, step, position):
        @pl.when((step < STEPS - 1) | (p % 2 == direction))
        def _():
            hop(direction, p, position, 1 + (step % 3) // 2).start()

        @pl.when(step % 3 == 2)
        def _():
            hop(direction, p, position, 1).start()

    for p in range(PIECES):
        for direction in both:
            hop(direction, p, 0, 1).start()

    row, col = iota((CHUNK, CHUNK + 128), 0), iota((CHUNK, CHUNK + 128), 1)
    upper_ref[...] = jnp.where((row < col) | (col >= CHUNK), 1.0, 0.0).astype(BF16)
    row, col = iota((BLOCKS * ROWS, PACKED), 0), iota((BLOCKS * ROWS, PACKED), 1)
    unpack = jnp.zeros((BLOCKS * ROWS, PACKED), F32)
    for j in range(BLOCKS):
        inside = (row >= ROWS * j) & (row < ROWS * j + CHANNELS)
        unpack = jnp.where(inside & (col == row - (ROWS - CHANNELS) * j), 1.0, unpack)
    unpack_ref[...] = unpack.astype(BF16)
    carry[...] = jnp.zeros_like(carry)
    early_acc[...] = jnp.zeros_like(early_acc)

    def build(lo, hi):
        @pl.loop(lo, hi)
        def _(j):
            build_tile(j, 0)
            build_tile(j, 1)
            place_chunk(j)

    def unpack_both(p, position):
        unpack_slots(p, [place_at(0, position), place_at(1, position)])

    spline_copy.wait()
    for p in range(PIECES):
        unpack_slots(p, [me_g])
    build(0, 2)

    @pl.loop(1, STEPS)
    def _(step):
        position = step + step // 3
        for group in range(2):
            pieces = (2 * group, 2 * group + 1)
            for p in pieces:
                for direction in both:
                    landed(direction, p, position)
                    send_step(direction, p, step, position)
            for p in pieces:
                unpack_both(p, position)

            @pl.when(step == 3)
            def _():
                for p in pieces:
                    for direction in both:
                        landed(direction, p, 3)
                    unpack_both(p, 3)

            turn_index = 2 * (step - 1) + group
            build(2 + (turn_index * 7) // 5, 2 + ((turn_index + 1) * 7) // 5)

    total = early_acc[0:4 * HIGH, :] + early_acc[4 * HIGH:, :]
    for c in range(4):
        for g in range(GRP):
            for top in range(2):
                start, source = 16 * g + 4 * c + 2 * top, HIGH * c + 2 * g
                early_out[start:start + 2, :] = total[source:source + 2, 128 * top:128 * top + 128]

    def far_group(n):
        return GRP // 2 + (n // 2) * (2 * (n % 2) - 1)

    def far_slab(n):
        def order(k):
            return (18 - k - k * (k - 1) // 2) % 4

        x, y = (me_s // 8 + order(n // 8)) % 4, ((me_s // 2) % 4 + order((n // 2) % 4)) % 4
        return x * 8 + y * 2 + (me_s + 1 + n) % 2

    def group_copy(source, landing, send, recv, j, arriving):
        peer = lax.rem(me_g + j, GRP)
        origin = peer if arriving else me_g
        flat = len(source.shape) == 2
        return pltpu.make_async_remote_copy(
            src_ref=source.at[pl.ds(pl.multiple_of(16 * peer, 16), 16)] if flat else source.at[peer],
            dst_ref=landing.at[pl.ds(pl.multiple_of(16 * origin, 16), 16)] if flat else landing.at[origin],
            send_sem=send.at[peer], recv_sem=recv.at[origin],
            device_id=(me_s, peer), device_id_type=MESH,
        )

    def slab_copy(source, landing, send, recv, j, arriving):
        peer = lax.rem(me_s + j, SLAB)
        origin = peer if arriving else me_s
        return pltpu.make_async_remote_copy(
            src_ref=source.at[pl.ds(pl.multiple_of(8 * peer, 8), 8)],
            dst_ref=landing.at[pl.ds(pl.multiple_of(8 * origin, 8), 8)],
            send_sem=send.at[peer], recv_sem=recv.at[origin],
            device_id=(peer, me_g), device_id_type=MESH,
        )

    def reduce_copy(buffer, send, recv, j, arriving, along_group):
        size = GRP if along_group else SLAB
        mine = me_g if along_group else me_s
        peer = lax.rem(mine + j, size)
        origin = peer if arriving else mine
        return pltpu.make_async_remote_copy(
            src_ref=buffer.at[origin], dst_ref=buffer.at[origin],
            send_sem=send.at[peer], recv_sem=recv.at[origin],
            device_id=(me_s, peer) if along_group else (peer, me_g), device_id_type=MESH,
        )

    def interpolate(j, half):
        rows = []
        for n in range(4):
            rows.append(
                jnp.concatenate(
                    [store[p, ids_ref[k, 4 * j + n]] for p in (2 * half, 2 * half + 1) for k in range(SLOTS)], axis=1
                )
            )
        crossed = jnp.dot(
            jnp.concatenate(rows, axis=0), tiles[j, 1024 * half:1024 * half + 1024], preferred_element_type=F32
        )
        left_block = iota((ROWS, 128), 1) < 64
        sides = []
        for side in range(2):
            part = crossed[2 * ROWS * side:2 * ROWS * side + 2 * ROWS, 128 * side:128 * side + 128]
            sides.append(jnp.where(left_block, part[:ROWS], part[ROWS:]))
        return jnp.concatenate(sides, axis=1)

    def last_pieces(pieces):
        for p in pieces:
            for direction in both:
                landed(direction, p, 7)
            unpack_both(p, 7)
        for p in pieces:
            landed(p % 2, p, 8)
            unpack_slots(p, [place_at(0, 8)])

    last_pieces((0, 1))

    @pl.loop(1, GRP)
    def _(j):
        group_copy(early_out, early1, e1s, e1r, far_group(j), False).start()

    mine = pl.ds(pl.multiple_of(16 * me_g, 16), 16)
    early1[mine, :] = early_out[mine, :]

    @pl.loop(0, CHUNKS, unroll=2)
    def _(j):
        first_half[:, pl.ds(pl.multiple_of(j * CHUNK, CHUNK), CHUNK)] = interpolate(j, 0)

    last_pieces((2, 3))

    gram_ref[...] = jnp.zeros_like(gram_ref)

    @pl.loop(0, CHUNKS, unroll=2)
    def _(j):
        lanes = pl.ds(pl.multiple_of(j * CHUNK, CHUNK), CHUNK)
        modelled = first_half[:, lanes] + interpolate(j, 1)
        weight = conf_ref[:, lanes]
        residual = meas_ref[:, lanes] - modelled[24:27]
        sens[:, lanes] = modelled[:24]
        resid[0:3, lanes] = residual
        left_side = jnp.concatenate(split_two(modelled[:24]), axis=0).astype(BF16)
        zeros = jnp.zeros((7, CHUNK), F32)
        weighted = jnp.concatenate(
            [
                piece
                for c in range(COMPS)
                for piece in (modelled[8 * c:8 * c + 8] * weight, residual[c:c + 1] * weight, zeros)
            ] + [jnp.zeros((16, CHUNK), F32)],
            axis=0,
        )
        right_side = jnp.concatenate(split_two(weighted), axis=0).astype(BF16)
        gram_ref[...] += lax.dot_general(
            left_side, right_side, (((1,), (1,)), ((), ())), preferred_element_type=F32
        )

    gram = gram_ref[...]
    gram = gram[:24] + gram[24:]
    gram = gram + pltpu.roll(gram, 64, 1)
    normal = gram[:8] + pltpu.roll(gram[8:16], 112, 1) + pltpu.roll(gram[16:24], 96, 1)
    sub, lane = iota((8, 128), 0), iota((8, 128), 1)
    normal = jnp.where(lane < 16, normal, 0.0)
    for shift in (16, 32, 64):
        normal = normal + pltpu.roll(normal, shift, 1)
    own_chunk = (lane >> 4) == sub
    red1[me_g] = jnp.sum(jnp.where(own_chunk, normal, 0.0), axis=0, keepdims=True)

    @pl.loop(1, GRP)
    def _(j):
        reduce_copy(red1, r1s, r1r, far_group(j), False, True).start()

    def turn(landing, outgoing, comps):
        for c in range(comps):
            for upper_part in range(4):
                for side in range(2):
                    if len(landing.shape) == 2:
                        block = landing[pl.ds(128 * side + 4 * c + upper_part, 8, stride=16), :]
                    else:
                        block = landing[8 * side:8 * side + 8, c, upper_part, :]
                    start = 64 * upper_part + 8 * (4 * side + c)
                    flip[start:start + 8, :] = swap_chunks(block)
        for upper_part in range(4):
            for lower_part in range(8):
                start = 64 * upper_part + 8 * lower_part
                outgoing[start:start + 8, :] = flip[pl.ds(64 * upper_part + lower_part, 8, stride=8), :]

    @pl.loop(1, GRP)
    def _(j):
        reduce_copy(red1, r1s, r1r, j, True, True).wait_recv()

    red2[me_s] = jnp.sum(red1[...], axis=0)

    @pl.loop(0, SLAB - 1)
    def _(j):
        reduce_copy(red2, r2s, r2r, far_slab(j) + SLAB - me_s, False, False).start()

    @pl.loop(1, SLAB)
    def _(j):
        reduce_copy(red2, r2s, r2r, j, True, False).wait_recv()

    system = jnp.where(own_chunk, jnp.sum(red2[...], axis=0), 0.0)
    for shift in (16, 32, 64):
        system = system + pltpu.roll(system, shift, 1)
    column = lane & 15
    system = jnp.where(column == sub, system * (1.0 + DAMPING), system)
    for i in range(PARAMS):
        factor = system[:, i:i + 1]
        pivot_row = system[i:i + 1, :] / system[i:i + 1, i:i + 1]
        system = jnp.where(sub == i, pivot_row, system - factor * pivot_row)
    update = system[:, 8:9]

    placed = jnp.zeros((6 * HIGH, LOW), F32)
    for q in range(8):
        lanes = slice(512 * q, 512 * (q + 1))
        mask = scatter_m[:, lanes]
        pieces = []
        for c in range(COMPS):
            predicted = jnp.sum(sens[8 * c:8 * c + 8, lanes] * update, axis=0, keepdims=True)
            pieces.append(split_two(resid[c:c + 1, lanes] - predicted))
        stacked = jnp.concatenate(
            [mask * pieces[c][part].astype(BF16) for part in range(2) for c in range(COMPS)], axis=0
        )
        placed = placed + jnp.dot(stacked, scatter_b[lanes, :], preferred_element_type=F32)
    placed = placed[:3 * HIGH] + placed[3 * HIGH:]
    for c in range(COMPS):
        for g in range(GRP):
            for top in range(2):
                source = HIGH * c + 2 * g
                late_out[g, c, 2 * top:2 * top + 2, :] = placed[source:source + 2, 128 * top:128 * top + 128]

    @pl.loop(1, GRP)
    def _(j):
        group_copy(late_out, late1, d1s, d1r, far_group(j), False).start()

    late1[me_g] = late_out[me_g]

    flat = jnp.sum(jnp.where(lane == sub, update, 0.0), axis=0, keepdims=True)
    upd_ref[...] = flat[:, :PARAMS]

    @pl.loop(1, GRP)
    def _(j):
        group_copy(early_out, early1, e1s, e1r, j, True).wait_recv()

    turn(early1, early2_out, 4)

    @pl.loop(0, SLAB - 1)
    def _(j):
        slab_copy(early2_out, early2, e2s, e2r, far_slab(j) + SLAB - me_s, False).start()

    own_rows = pl.ds(pl.multiple_of(8 * me_s, 8), 8)
    early2[own_rows, :] = early2_out[own_rows, :]

    @pl.loop(1, GRP)
    def _(j):
        group_copy(late_out, late1, d1s, d1r, j, True).wait_recv()

    turn(late1, late2_out, 3)

    @pl.loop(0, SLAB - 1)
    def _(j):
        slab_copy(late2_out, late2, d2s, d2r, far_slab(j) + SLAB - me_s, False).start()

    late2[own_rows, :] = late2_out[own_rows, :]

    @pl.loop(1, SLAB)
    def _(j):
        slab_copy(early2_out, early2, e2s, e2r, j, True).wait_recv()

    @pl.loop(1, SLAB)
    def _(j):
        slab_copy(late2_out, late2, d2s, d2r, j, True).wait_recv()

    for first in range(0, SLAB, 8):
        for side in range(2):
            def rows_of(ref, c):
                return ref[pl.ds(8 * first + 4 * side + c, 8, stride=8), :]

            confidence = rows_of(early2, 3)
            squares = jnp.zeros_like(confidence)
            results = []
            late_rows = [rows_of(late2, c) for c in range(COMPS)]
            for c in range(COMPS):
                results.append(rows_of(early2, c) - late_rows[c])
            for c in range(COMPS):
                results.append(confidence * late_rows[c])
                squares = squares + late_rows[c] * late_rows[c]
            results.append(confidence)
            results.append(confidence * squares)
            for r in range(8):
                flip[8 * r:8 * r + 8, :] = results[r]
            for n in range(8):
                start = 256 * (first + n) + 128 * side
                out_ref[:, start:start + 128] = flip[pl.ds(n, 8, stride=8), :]

    for p in range(PIECES):
        for direction in both:
            @pl.loop(1, 9 if p % 2 == direction else 8)
            def _(position):
                hop(direction, p, position - 1, 1).wait_send()

    @pl.loop(1, GRP)
    def _(j):
        group_copy(early_out, early1, e1s, e1r, j, False).wait_send()
        group_copy(late_out, late1, d1s, d1r, j, False).wait_send()
        reduce_copy(red1, r1s, r1r, j, False, True).wait_send()

    @pl.loop(1, SLAB)
    def _(j):
        slab_copy(early2_out, early2, e2s, e2r, j, False).wait_send()
        slab_copy(late2_out, late2, d2s, d2r, j, False).wait_send()
        reduce_copy(red2, r2s, r2r, j, False, False).wait_send()


def body(fields, spline, measured, confidence, block_ids, live, owners):
    vmem = pl.BlockSpec(memory_space=pltpu.VMEM)
    smem = pl.BlockSpec(memory_space=pltpu.SMEM)
    dma = pltpu.SemaphoreType.DMA
    received, update = pl.pallas_call(
        kernel,
        out_shape=(
            jax.ShapeDtypeStruct((8, PEERS * CAP), F32),
            jax.ShapeDtypeStruct((1, PARAMS), F32),
        ),
        in_specs=[smem, smem, vmem, pl.BlockSpec(memory_space=pl.ANY), vmem, vmem, vmem],
        out_specs=(vmem, vmem),
        scratch_shapes=[
            pltpu.VMEM((3, 8, SLOTS, SUBSETS), BF16),
            dma,
            pltpu.VMEM((PIECES, GRP, PACKED, PIECE), BF16),
            pltpu.VMEM((PIECES, GRP * BLOCKS, ROWS, PIECE), BF16),
            pltpu.VMEM((CHUNKS, SLOTS * BLK, CHUNK), BF16),
            pltpu.VMEM((3, 32, 128), F32),
            pltpu.VMEM((PEERS, 128), F32),
            pltpu.VMEM((CHUNK, CHUNK + 128), BF16),
            pltpu.VMEM((BLOCKS * ROWS, PACKED), BF16),
            pltpu.VMEM((SUBSETS, LOW), BF16),
            pltpu.VMEM((HIGH, SUBSETS), BF16),
            pltpu.VMEM((8 * HIGH, LOW), F32),
            pltpu.VMEM((ROWS, SUBSETS), F32),
            pltpu.VMEM((24, SUBSETS), F32),
            pltpu.VMEM((8, SUBSETS), F32),
            pltpu.VMEM((48, 128), F32),
            pltpu.VMEM((GRP, 1, 128), F32),
            pltpu.VMEM((SLAB, 1, 128), F32),
            pltpu.VMEM((GRP * 16, 128), F32),
            pltpu.VMEM((GRP * 16, 128), F32),
            pltpu.VMEM((SLAB * 8, 128), F32),
            pltpu.VMEM((SLAB * 8, 128), F32),
            pltpu.VMEM((GRP, COMPS, 4, 128), F32),
            pltpu.VMEM((GRP, COMPS, 4, 128), F32),
            pltpu.VMEM((SLAB * 8, 128), F32),
            pltpu.VMEM((SLAB * 8, 128), F32),
            pltpu.VMEM((256, 128), F32),
            dma((2, PIECES, 9)), dma((2, PIECES, 9)),
            dma((GRP,)), dma((GRP,)), dma((SLAB,)), dma((SLAB,)),
            dma((GRP,)), dma((GRP,)), dma((SLAB,)), dma((SLAB,)),
            dma((GRP,)), dma((GRP,)), dma((SLAB,)), dma((SLAB,)),
        ],
        compiler_params=pltpu.CompilerParams(
            collective_id=0, has_side_effects=True, vmem_limit_bytes=56 * 1024 * 1024
        ),
    )(
        block_ids.T, live, fields, spline, measured,
        confidence.reshape(1, SUBSETS), owners.reshape(1, SUBSETS),
    )
    return (received, update.reshape(PARAMS))


def solution(mesh):
    placed = (
        P(None, ("slab", "grp")),
        P(None, None, None, ("slab", "grp")),
        P(None, ("slab", "grp")),
        P(("slab", "grp")),
        P(("slab", "grp"), None),
        P(("slab", "grp")),
        P(("slab", "grp"), None),
    )
    return jax.shard_map(
        body, mesh=mesh, in_specs=placed, out_specs=(P(None, ("slab", "grp")), P()), check_vma=False
    )
```
